32 devices in a mesh: seq: 4 (over x, core), blk: 8 (over z, y).
Axes of the slice: x: 2, y: 2, z: 4, core: 2. Of those that a mesh axis runs over, the one named last changes fastest.
Arguments:
- residual_in: bfloat16 [8, 512, 2048], P('blk', 'seq'), may hold values from -6 to 6
- segment_ids: int32 [8, 512], P('blk'), may hold values from 0 to 2, never falling along the last dimension, each value on 1 to 256 neighbouring positions
- attn_gain: bfloat16 [2048], replicated, may hold values from 0.5 to 1.5
- w_qkv: bfloat16 [2048, 16, 384], P(None, 'seq')
- w_out: bfloat16 [16, 128, 2048], P('seq'), may hold values from -0.125 to 0.125
- ffn_gain: bfloat16 [2048], replicated, may hold values from 0.5 to 1.5
- w_router: bfloat16 [2048, 8], replicated, may hold values from -0.125 to 0.125
- routes: int32 [8, 512, 2], P('blk', 'seq'), may hold values from 0 to 7, all different within a row; in each aligned block of 128 rows (0 to 127, 128 to 255, ..., all dimensions but the last counted through in order) at most 48 rows name the same one
- w_gate_up: bfloat16 [8, 2048, 2048], P('blk'), may hold values from -0.125 to 0.125
- w_down: bfloat16 [8, 1024, 2048], P('blk'), may hold values from -0.1875 to 0.1875
- page_owner: int32 [8, 8], P('blk'), may hold values from 0 to 7, each once within a row
Outputs:
- residual_out: bfloat16 [8, 512, 2048], P('blk', 'seq')
- kv_cache: bfloat16 [8, 8, 64, 4096], P('blk', None, None, 'seq')
The draws below stay inside these ranges and needn't reach their ends.
Inputs may be any that keep to these rules, and one draw needn't show every extreme that they name: `segment_ids`: within a pack the numbers never fall; 1 to 3 prompts a pack, the longest exactly 256 tokens. `routes`: each token names 2 different experts; among the 128 tokens of one device no expert is named more than 48 times, a bound that some block reaches. `page_owner`: each row is a permutation.
All inputs are finite; a program needn't handle non-finite values.
Results may differ from the reference program's by a relative error of at most 0.025.
Values may be sent and summed in bfloat16 or wider, within the bound.
No kernel may reach another device: no remote copies, remote signals or barrier semaphores. Data moves between devices by JAX's collectives and lax.ppermute only.
A program may use at most 128 MiB of HBM per device.

```python
import math
import jax
import jax.numpy as jnp
import numpy as np
from jax import lax

D = 2048
HEADS = 16
HD = 128
FF = 1024
EXPERTS = 8
TOP = 2
TOK_DEV = 128
GROUP_TOK = 512
CAP = 48
PAGE = 64
N_BLK = 8


def draw_w_qkv(key, part):
    base_key = jax.random.fold_in(jax.random.fold_in(key, 11), 0)
    base = jax.random.normal(base_key, (D, HEADS, 3 * HD), jnp.float32) / math.sqrt(D)
    return base.astype(jnp.bfloat16)


def block_scale(key, shape, cuts, smallest, largest):
    level = 1.0
    for position, blocks in cuts:
        draws = jax.random.uniform(jax.random.fold_in(jax.random.fold_in(key, 6), position), (blocks,), jnp.float32, smallest / len(cuts), largest / len(cuts))
        level = level * jnp.repeat(jnp.exp(draws), shape[position] // blocks).reshape((-1,) + (1,) * (len(shape) - 1 - position))
    return level


def split_up(count, total, limit, skew):
    weights = [(1 << 20) // math.isqrt(grade ** skew) + 1 for grade in range(2, count + 1)]
    rest, counts = total - limit - (count - 1), [1] * (count - 1)
    while rest > 0:
        movable = [i for i in range(count - 1) if counts[i] < limit]
        pool, budget = sum([weights[i] for i in movable]), rest
        for i in movable:
            more = min(limit - counts[i], max(1, budget * weights[i] // pool), rest)
            counts[i] = counts[i] + more
            rest = rest - more
    return np.array([limit] + counts)


def ragged_sizes(rng, number_of, total, bound, lean):
    if number_of == 2:
        one = jax.random.randint(rng, (), max(1, total - bound), min(bound, total - 1) + 1)
        return jnp.stack([one, total - one])
    lengths = jnp.asarray(split_up(number_of, total, bound, lean), jnp.int32)
    couples = (number_of - 1) // 2
    donor, taker = lengths[1:1 + 2 * couples:2], lengths[2:2 + 2 * couples:2]
    room = jnp.minimum(donor - 1, bound - taker)
    moved = jax.random.randint(jax.random.fold_in(rng, 1), (couples,), 0, 1 << 20) % (room + 1)
    lengths = lengths.at[1:1 + 2 * couples:2].set(donor - moved).at[2:2 + 2 * couples:2].set(taker + moved)
    return lengths[jax.random.permutation(jax.random.fold_in(rng, 2), number_of)]


def routed_block(own_key, own, number, rows, number_of, top, bound, lean):
    ranking = jax.random.permutation(own_key, number_of)
    heavy_load, common = load_shares(number_of, rows * top, bound, lean, True), load_shares(number_of, rows * top, bound, lean, False)
    places = jnp.arange(number_of)

    def named(lengths, offset_by):
        used = int((lengths > 0).sum())
        fixed = max(1, used // 4)
        passed = fixed + (places - fixed + offset_by * (used - fixed)) % max(1, number_of - fixed)
        return jnp.zeros((number_of,), jnp.int32).at[ranking[jnp.where(places < fixed, places, passed)]].set(jnp.asarray(lengths, jnp.int32))

    lengths = jnp.where(number % 4 == 0, named(heavy_load, number // 4), named(common, number - number // 4 - 1))
    mixed = jax.random.permutation(jax.random.fold_in(own, 3), number_of)
    giver, receiver = mixed[0:number_of // 2 * 2:2], mixed[1:number_of // 2 * 2:2]
    margin = jnp.minimum(lengths[giver] - 1, bound - lengths[receiver]) // 2
    margin = jnp.where((giver == ranking[0]) | (receiver == ranking[0]) | (lengths[receiver] == 0), 0, jnp.maximum(margin, 0))
    passed = jax.random.randint(jax.random.fold_in(own, 4), (number_of // 2,), 0, 1 << 20) % (margin + 1)
    lengths = lengths.at[giver].add(-passed).at[receiver].add(passed)
    items = jnp.searchsorted(jnp.cumsum(lengths), jnp.arange(rows * top), side="right").astype(jnp.int32)
    table = items.reshape(top, rows).T
    table = table[jax.random.permutation(jax.random.fold_in(own, 1), rows)]
    offset_by = jax.random.randint(jax.random.fold_in(own, 2), (rows, 1), 0, top)
    return jnp.take_along_axis(table, (jnp.arange(top)[None, :] + offset_by) % top, axis=1)


def load_shares(number_of, total, bound, slope, full):
    weights = [(1 << 20) // math.isqrt(rank ** slope) + 1 for rank in range(1, number_of + 1)]
    largest = bound if full else min(bound, max(-(-total // number_of), total * weights[0] // sum(weights)))
    least = 1 if total - largest >= number_of - 1 else 0
    holding, surplus = [largest] + [least] * (number_of - 1), total - largest - least * (number_of - 1)
    while surplus > 0:
        movable = [i for i in range(1, number_of) if holding[i] < largest] or [i for i in range(1, number_of) if holding[i] < bound]
        pool, remaining = sum([weights[i] for i in movable]), surplus
        for i in movable:
            more = min(bound - holding[i], max(1, remaining * weights[i] // pool), surplus)
            holding[i] = holding[i] + more
            surplus = surplus - more
    return np.array(holding)


def bell_draw(rng, shape, scale, limit, pieces=(), kind=jnp.bfloat16):
    drawn = scale * jax.random.normal(rng, shape, jnp.float32)
    if pieces:
        drawn = drawn * block_scale(rng, shape, pieces, -0.22, 0.18)
    return jnp.clip(drawn, -limit, limit).astype(kind)


def setup_inputs(seed: int = 0) -> dict:
    arg_keys = jax.random.split(jax.random.key(seed), 12)
    residual_in = bell_draw(arg_keys[0], (N_BLK, GROUP_TOK, D), 1.0, 6.0, ((0, 8), (1, 4)))
    segment_ids = jax.vmap(lambda own: jnp.searchsorted(jnp.cumsum(ragged_sizes(own, 3, GROUP_TOK, GROUP_TOK // 2, 2)), jnp.arange(GROUP_TOK), side="right"))(jax.random.split(arg_keys[1], N_BLK)).reshape((N_BLK, GROUP_TOK)).astype(jnp.int32)
    attn_gain = jnp.clip(1.0 + 0.1 * jax.random.normal(arg_keys[2], (D,), jnp.float32), 0.5, 1.5).astype(jnp.bfloat16)
    w_qkv = draw_w_qkv(jax.random.fold_in(arg_keys[11], 71), 0)
    w_out = bell_draw(arg_keys[4], (HEADS, HD, D), (HEADS * HD) ** -0.5, 0.125, ((0, 4),))
    ffn_gain = jnp.clip(1.0 + 0.1 * jax.random.normal(arg_keys[5], (D,), jnp.float32), 0.5, 1.5).astype(jnp.bfloat16)
    w_router = bell_draw(arg_keys[6], (D, EXPERTS), D ** -0.5, 0.125)
    routes_keys = jax.random.split(jax.random.fold_in(arg_keys[7], 1), N_BLK * GROUP_TOK // TOK_DEV)
    routes_turns = jax.random.permutation(jax.random.fold_in(arg_keys[7], 3), N_BLK * GROUP_TOK // TOK_DEV)
    routes = jax.vmap(lambda own, number: routed_block(jax.random.fold_in(arg_keys[7], 2), own, number, TOK_DEV, EXPERTS, TOP, CAP, 2))(routes_keys, routes_turns).reshape((N_BLK, GROUP_TOK, TOP))
    w_gate_up = bell_draw(arg_keys[8], (EXPERTS, D, 2 * FF), D ** -0.5, 0.125, ((0, 8),))
    w_down = bell_draw(arg_keys[9], (EXPERTS, FF, D), FF ** -0.5, 0.1875, ((0, 8),))
    page_owner = jax.vmap(lambda own: jax.random.permutation(own, N_BLK))(jax.random.split(arg_keys[10], N_BLK)).reshape((N_BLK, N_BLK)).astype(jnp.int32)
    return {"residual_in": residual_in, "segment_ids": segment_ids, "attn_gain": attn_gain, "w_qkv": w_qkv, "w_out": w_out, "ffn_gain": ffn_gain, "w_router": w_router, "routes": routes, "w_gate_up": w_gate_up, "w_down": w_down, "page_owner": page_owner}


EPS = 1e-06

def rms_norm(value, gain):
    wide = value.astype(jnp.float32)
    scale = lax.rsqrt(lax.optimization_barrier(jnp.mean(wide * wide, axis=-1, keepdims=True)) + EPS)
    return (wide * scale * gain.astype(jnp.float32)).astype(jnp.bfloat16)

def reference(residual_in, segment_ids, attn_gain, w_qkv, w_out, ffn_gain, w_router, routes, w_gate_up, w_down, page_owner):
    w_flat = w_qkv.reshape(D, HEADS * 3 * HD)
    w_out_flat = w_out.reshape(HEADS * HD, D)

    def one_group(pair):
        rows, segment_row = pair
        normed = rms_norm(rows, attn_gain)
        qkv = jnp.dot(normed, w_flat, preferred_element_type=jnp.float32).astype(jnp.bfloat16)
        qkv = qkv.reshape(GROUP_TOK, HEADS, 3 * HD)
        query = qkv[:, :, :HD].astype(jnp.float32)
        key = qkv[:, :, HD:2 * HD].astype(jnp.float32)
        value = qkv[:, :, 2 * HD:].astype(jnp.float32)
        scores = jnp.einsum('qhd,khd->hqk', query, key) / math.sqrt(HD)
        same = segment_row[:, None] == segment_row[None, :]
        scores = jnp.where(same[None], scores, jnp.float32(-1e+30))
        top = lax.optimization_barrier(jnp.max(scores, axis=-1, keepdims=True))
        weights = jnp.exp(scores - top)
        probs = (weights / lax.optimization_barrier(jnp.sum(weights, axis=-1, keepdims=True))).astype(jnp.bfloat16)
        context = jnp.einsum('hqk,khd->qhd', probs.astype(jnp.float32), value).astype(jnp.bfloat16)
        mixed = jnp.dot(context.reshape(GROUP_TOK, HEADS * HD), w_out_flat, preferred_element_type=jnp.float32)
        resid = (rows.astype(jnp.float32) + mixed).astype(jnp.bfloat16)
        kv_rows = qkv[:, :, HD:].reshape(GROUP_TOK, HEADS * 2 * HD)
        return (resid, kv_rows)
    resid, kv_rows = lax.map(one_group, (residual_in, segment_ids))
    pages = kv_rows.reshape(N_BLK, N_BLK, PAGE, HEADS * 2 * HD)
    kv_cache = jnp.zeros((N_BLK, N_BLK, PAGE, HEADS * 2 * HD), jnp.bfloat16)
    kv_cache = kv_cache.at[page_owner, jnp.arange(N_BLK, dtype=jnp.int32)[:, None]].set(pages)
    tokens = resid.reshape(N_BLK * GROUP_TOK, D)
    ffn_in = rms_norm(tokens, ffn_gain)
    logits = jnp.dot(ffn_in, w_router, preferred_element_type=jnp.float32)
    gates = jax.nn.sigmoid(logits).astype(jnp.bfloat16)
    route_flat = routes.reshape(-1, TOP)
    expert_ids = jnp.arange(EXPERTS, dtype=jnp.int32)
    chosen = jnp.any(route_flat[:, :, None] == expert_ids[None, None, :], axis=1)
    blocks = chosen.reshape(-1, TOK_DEV, EXPERTS).astype(jnp.int32)
    rank = jnp.cumsum(blocks, axis=1) - 1
    block_count = blocks.shape[0]
    slot_ids = jnp.arange(CAP, dtype=jnp.int32)
    row_ids = jnp.arange(TOK_DEV, dtype=jnp.int32)
    block_ids = jnp.arange(block_count, dtype=jnp.int32)

    def one_expert(total, expert):
        mask_e = blocks[:, :, expert]
        rank_e = rank[:, :, expert]
        hit = (mask_e[:, None, :] == 1) & (rank_e[:, None, :] == slot_ids[None, :, None])
        slot_row = lax.optimization_barrier(jnp.sum(jnp.where(hit, row_ids[None, None, :], 0), axis=2)).astype(jnp.int32)
        pick = (block_ids[:, None] * TOK_DEV + slot_row).reshape(-1).astype(jnp.int32)
        picked = jnp.take(ffn_in, pick, axis=0)
        both = jnp.dot(picked, w_gate_up[expert], preferred_element_type=jnp.float32)
        hidden = (jax.nn.silu(both[:, :FF]) * both[:, FF:]).astype(jnp.bfloat16)
        output = jnp.dot(hidden, w_down[expert], preferred_element_type=jnp.float32)
        back = (block_ids[:, None] * CAP + jnp.clip(rank_e, 0, CAP - 1)).reshape(-1).astype(jnp.int32)
        per_row = jnp.take(output, back, axis=0)
        contrib = (gates[:, expert].astype(jnp.float32)[:, None] * per_row).astype(jnp.bfloat16)
        live = mask_e.reshape(-1)[:, None] == 1
        total = total + jnp.where(live, contrib.astype(jnp.float32), jnp.float32(0.0))
        return (total, None)
    total, _ = lax.scan(one_expert, jnp.zeros((N_BLK * GROUP_TOK, D), jnp.float32), expert_ids)
    residual_out = (tokens.astype(jnp.float32) + total).astype(jnp.bfloat16).reshape(N_BLK, GROUP_TOK, D)
    return (residual_out, kv_cache)
```

```python
import math

import jax
import jax.numpy as jnp
from jax import lax
from jax.sharding import PartitionSpec as P

EPS = 1e-06


def rms_norm(value, gain):
    wide = value.astype(jnp.float32)
    scale = lax.rsqrt(jnp.mean(wide * wide, axis=-1, keepdims=True) + EPS)
    return (wide * scale * gain.astype(jnp.float32)).astype(jnp.bfloat16)


def swap(value, axis, step):
    size = lax.axis_size(axis)
    return lax.ppermute(value, axis, [(i, i ^ step) for i in range(size)])


def on_device(
    residual_in,
    segment_ids,
    attn_gain,
    w_qkv,
    w_out,
    ffn_gain,
    w_router,
    routes,
    w_gate_up,
    w_down,
    page_owner,
):
    own = residual_in[0]
    tok_dev, width = own.shape
    heads_here = w_qkv.shape[1]
    head_dim = w_out.shape[1]
    seq_count = lax.axis_size("seq")
    blk_count = lax.axis_size("blk")
    seq_me = lax.axis_index("seq")
    blk_me = lax.axis_index("blk")
    seq_steps = jnp.arange(seq_count, dtype=jnp.int32)
    blk_steps = jnp.arange(blk_count, dtype=jnp.int32)

    core = swap(own, "seq", 1)
    far = swap(own, "seq", 2)
    far_core = swap(far, "seq", 1)

    capacity = tok_dev * 3 // 8
    route_rows = routes[0]
    experts = blk_me ^ blk_steps
    chosen = jnp.any(route_rows[:, :, None] == experts[None, None, :], axis=1)
    rank = jnp.cumsum(chosen.astype(jnp.int32), axis=0) - 1
    slot = jnp.where(chosen, rank, -1)
    slots = jnp.arange(capacity, dtype=jnp.int32)
    hit = slot.T[:, None, :] == slots[None, :, None]
    pick = hit.astype(jnp.bfloat16).reshape(blk_count * capacity, tok_dev)

    w_flat = w_qkv.reshape(width, heads_here * 3 * head_dim)

    def project(rows):
        return jnp.dot(
            rms_norm(rows, attn_gain), w_flat, preferred_element_type=jnp.float32
        ).astype(jnp.bfloat16)

    qkv = jnp.concatenate(
        [
            project(jnp.concatenate([own, core], axis=0)),
            project(jnp.concatenate([far, far_core], axis=0)),
        ],
        axis=0,
    )
    group_len = qkv.shape[0]
    segment_row = jnp.take(
        segment_ids[0].reshape(seq_count, tok_dev), seq_me ^ seq_steps, axis=0
    ).reshape(group_len)

    page_len = group_len // blk_count
    per_dev = tok_dev // page_len
    qkv_heads = qkv.reshape(group_len, heads_here, 3 * head_dim)
    kv_rows = qkv_heads[:, :, head_dim:].reshape(blk_count, page_len, heads_here * 2 * head_dim)
    owners = page_owner[0]
    page_of = jnp.sum(
        jnp.where(owners[None, :] == experts[:, None], blk_steps[None, :], 0), axis=1
    )
    place = ((page_of // per_dev) ^ seq_me) * per_dev + page_of % per_dev
    outgoing = jnp.take(kv_rows, place, axis=0)
    arrived = jnp.stack(
        [outgoing[0]] + [swap(outgoing[s], "blk", s) for s in range(1, blk_count)]
    )
    kv_cache = jnp.take(arrived, experts, axis=0)[None]

    query = qkv_heads[:, :, :head_dim]
    key_rows = qkv_heads[:, :, head_dim : 2 * head_dim]
    value_rows = qkv_heads[:, :, 2 * head_dim :]
    scores = jnp.einsum(
        "qhd,khd->hqk", query, key_rows, preferred_element_type=jnp.float32
    ) / math.sqrt(head_dim)
    same = segment_row[:, None] == segment_row[None, :]
    scores = jnp.where(same[None], scores, jnp.float32(-1e30))
    top = jnp.max(scores, axis=-1, keepdims=True)
    weights = jnp.exp(scores - top)
    probs = (weights / jnp.sum(weights, axis=-1, keepdims=True)).astype(jnp.bfloat16)
    context = jnp.einsum(
        "hqk,khd->qhd", probs, value_rows, preferred_element_type=jnp.float32
    ).astype(jnp.bfloat16)
    context_flat = context.reshape(group_len, heads_here * head_dim)
    w_out_flat = w_out.reshape(heads_here * head_dim, width)
    mixed = jnp.dot(context_flat, w_out_flat, preferred_element_type=jnp.float32)
    parts = mixed.astype(jnp.bfloat16).reshape(seq_count, tok_dev, width)

    here = parts[3]
    far_sum = (parts[2].astype(jnp.float32) + swap(here, "seq", 1).astype(jnp.float32)).astype(
        jnp.bfloat16
    )
    from_core = swap(parts[1], "seq", 1)
    from_far = swap(far_sum, "seq", 2)
    resid = (
        own.astype(jnp.float32)
        + (mixed[:tok_dev] + from_core.astype(jnp.float32))
        + from_far.astype(jnp.float32)
    ).astype(jnp.bfloat16)

    ffn_in = rms_norm(resid, ffn_gain)
    sent = jnp.dot(pick, ffn_in, preferred_element_type=jnp.float32).astype(jnp.bfloat16)
    sent = sent.reshape(blk_count, capacity, width)
    rows = jnp.concatenate(
        [sent[0]] + [swap(sent[s], "blk", s) for s in range(1, blk_count)], axis=0
    )

    gates = jax.nn.sigmoid(jnp.dot(ffn_in, w_router, preferred_element_type=jnp.float32)).astype(
        jnp.bfloat16
    )
    expert_ids = jnp.arange(w_router.shape[1], dtype=jnp.int32)
    gate_of = jnp.sum(
        jnp.where(experts[:, None, None] == expert_ids[None, None, :], gates[None], 0), axis=2
    ).astype(jnp.bfloat16)
    weigh = jnp.where(hit, gate_of[:, None, :], 0).reshape(blk_count * capacity, tok_dev)

    gate_up = w_gate_up[0]
    down = w_down[0]
    ff_width = down.shape[0]
    both = jnp.dot(rows, gate_up, preferred_element_type=jnp.float32)
    hidden = (jax.nn.silu(both[:, :ff_width]) * both[:, ff_width:]).astype(jnp.bfloat16)
    output = jnp.dot(hidden, down, preferred_element_type=jnp.float32).astype(jnp.bfloat16)
    output = output.reshape(blk_count, capacity, width)
    back = jnp.concatenate(
        [output[0]] + [swap(output[s], "blk", s) for s in range(1, blk_count)], axis=0
    )
    total = lax.dot_general(
        weigh, back, (((0,), (0,)), ((), ())), preferred_element_type=jnp.float32
    )
    residual_out = (resid.astype(jnp.float32) + total).astype(jnp.bfloat16)[None]
    return (residual_out, kv_cache)


def solution(mesh):
    in_specs = (
        P("blk", "seq", None),
        P("blk", None),
        P(),
        P(None, "seq", None),
        P("seq", None, None),
        P(),
        P(),
        P("blk", "seq", None),
        P("blk", None, None),
        P("blk", None, None),
        P("blk", None),
    )
    out_specs = (P("blk", "seq", None), P("blk", None, None, "seq"))
    return jax.shard_map(
        on_device, mesh=mesh, in_specs=in_specs, out_specs=out_specs, check_vma=False
    )
```

```python
import functools
import math

import jax
import jax.numpy as jnp
from jax import lax
from jax.experimental import pallas as pl
from jax.experimental.pallas import tpu as pltpu
from jax.sharding import PartitionSpec as P

EPS = 1e-06
F32 = jnp.float32
BF16 = jnp.bfloat16
MIB = 1 << 20


def rms_norm(value, gain):
    wide = value.astype(F32)
    scale = lax.rsqrt(jnp.mean(wide * wide, axis=-1, keepdims=True) + EPS)
    return (wide * scale * gain.astype(F32)).astype(BF16)


def swap(value, axis, step):
    size = lax.axis_size(axis)
    return lax.ppermute(value, axis, [(i, i ^ step) for i in range(size)])


def whole(shape):
    return pl.BlockSpec(shape, lambda *_: (0,) * len(shape))


def params(mib):
    return pltpu.CompilerParams(vmem_limit_bytes=mib * MIB)


def cost(flops, bytes_accessed):
    return pl.CostEstimate(flops=flops, bytes_accessed=bytes_accessed, transcendentals=0)


def project_kernel(a_ref, b_ref, gain_ref, w_ref, q_ref, kv_ref, normed):
    rows = a_ref.shape[0]
    head_dim = q_ref.shape[1]

    @pl.when(pl.program_id(0) == 0)
    def _():
        normed[:rows] = rms_norm(a_ref[...], gain_ref[...])
        normed[rows:] = rms_norm(b_ref[...], gain_ref[...])

    out = jnp.dot(normed[...], w_ref[...], preferred_element_type=F32).astype(BF16)
    q_ref[...] = out[:, :head_dim]
    kv_ref[...] = out[:, head_dim:]


def project(a, b, gain, w_flat, heads, head_dim):
    rows, width = a.shape
    return pl.pallas_call(
        project_kernel,
        grid=(heads,),
        out_shape=(
            jax.ShapeDtypeStruct((2 * rows, heads * head_dim), BF16),
            jax.ShapeDtypeStruct((2 * rows, heads * 2 * head_dim), BF16),
        ),
        in_specs=[
            whole((rows, width)),
            whole((rows, width)),
            whole((1, width)),
            pl.BlockSpec((width, 3 * head_dim), lambda h: (0, h)),
        ],
        out_specs=(
            pl.BlockSpec((2 * rows, head_dim), lambda h: (0, h)),
            pl.BlockSpec((2 * rows, 2 * head_dim), lambda h: (0, h)),
        ),
        scratch_shapes=[pltpu.VMEM((2 * rows, width), BF16)],
        compiler_params=params(24),
        cost_estimate=cost(2 * 2 * rows * width * 3 * heads * head_dim, w_flat.size * 2),
        name="project",
    )(a, b, gain, w_flat)


def pages_out_kernel(place_ref, near_ref, far_ref, *refs):
    outs, sems = refs[:-1], refs[-1]
    page_len = outs[0].shape[0]
    pages_near = near_ref.shape[0] // page_len
    for s, out in enumerate(outs):
        place = place_ref[s]

        @pl.when(place < pages_near)
        def _(place=place, out=out, s=s):
            start = pl.multiple_of(place * page_len, page_len)
            pltpu.make_async_copy(near_ref.at[pl.ds(start, page_len)], out, sems.at[s]).start()

        @pl.when(place >= pages_near)
        def _(place=place, out=out, s=s):
            start = pl.multiple_of((place - pages_near) * page_len, page_len)
            pltpu.make_async_copy(far_ref.at[pl.ds(start, page_len)], out, sems.at[s]).start()

    for s, out in enumerate(outs):
        pltpu.make_async_copy(near_ref.at[pl.ds(0, page_len)], out, sems.at[s]).wait()


def pages_out(place, near, far, count):
    page_len = 2 * near.shape[0] // count
    shape = jax.ShapeDtypeStruct((page_len, near.shape[1]), BF16)
    any_spec = pl.BlockSpec(memory_space=pl.ANY)
    return pl.pallas_call(
        pages_out_kernel,
        out_shape=(shape,) * count,
        in_specs=[pl.BlockSpec(memory_space=pltpu.SMEM), any_spec, any_spec],
        out_specs=(any_spec,) * count,
        scratch_shapes=[pltpu.SemaphoreType.DMA((count,))],
        cost_estimate=cost(0, 4 * near.size * 2),
        name="pages_out",
    )(place, near, far)


def pages_in_kernel(slot_ref, *refs):
    pages, out, sems = refs[:-2], refs[-2], refs[-1]
    copies = [
        pltpu.make_async_copy(page, out.at[0, slot_ref[s]], sems.at[s])
        for s, page in enumerate(pages)
    ]
    for copy in copies:
        copy.start()
    for copy in copies:
        copy.wait()


def pages_in(slot, pages):
    count = len(pages)
    any_spec = pl.BlockSpec(memory_space=pl.ANY)
    return pl.pallas_call(
        pages_in_kernel,
        out_shape=jax.ShapeDtypeStruct((1, count) + pages[0].shape, BF16),
        in_specs=[pl.BlockSpec(memory_space=pltpu.SMEM)] + [any_spec] * count,
        out_specs=any_spec,
        scratch_shapes=[pltpu.SemaphoreType.DMA((count,))],
        cost_estimate=cost(0, 4 * count * pages[0].size),
        name="pages_in",
    )(slot, *pages)


def attend_kernel(
    col_ref, row_ref, q_near, q_far, kv_near, kv_far, keep_ref, send_ref, bias, *, head_dim
):
    half = q_near.shape[0]
    block = half // 2
    factor = math.log2(math.e) / math.sqrt(head_dim)
    bias[...] = jnp.where(col_ref[...] == row_ref[...], F32(0), F32(-1e30))
    for h in range(q_near.shape[1] // head_dim):
        q_cols = slice(h * head_dim, (h + 1) * head_dim)
        k_cols = slice(2 * h * head_dim, (2 * h + 1) * head_dim)
        v_cols = slice((2 * h + 1) * head_dim, (2 * h + 2) * head_dim)
        key = jnp.concatenate([kv_near[:, k_cols], kv_far[:, k_cols]], axis=0)
        value = jnp.concatenate([kv_near[:, v_cols], kv_far[:, v_cols]], axis=0)
        for part, q_ref in enumerate((q_near, q_far)):
            scores = lax.dot_general(
                q_ref[:, q_cols], key, (((1,), (1,)), ((), ())), preferred_element_type=F32
            )
            scores = scores + bias[part * half : (part + 1) * half]
            top = jnp.max(scores, axis=-1, keepdims=True)
            weights = jnp.exp2((scores - top) * factor)
            total = jnp.sum(weights, axis=-1, keepdims=True)
            context = jnp.dot(weights.astype(BF16), value, preferred_element_type=F32)
            context = (context / total).astype(BF16)
            rows = slice(part * block, (part + 1) * block)
            keep_ref[rows, q_cols] = context[:block]
            send_ref[rows, q_cols] = context[block:]


def attend(segment_row, q_near, q_far, kv_near, kv_far, head_dim):
    group_len = segment_row.shape[0]
    half = q_near.shape[0]
    cols = q_near.shape[1]
    shape = jax.ShapeDtypeStruct((half, cols), BF16)
    return pl.pallas_call(
        functools.partial(attend_kernel, head_dim=head_dim),
        out_shape=(shape, shape),
        scratch_shapes=[pltpu.VMEM((group_len, group_len), F32)],
        compiler_params=params(32),
        cost_estimate=cost(4 * group_len * group_len * cols, 6 * q_near.size * 2),
        name="attend",
    )(segment_row[:, None], segment_row[None, :], q_near, q_far, kv_near, kv_far)


def out_project_kernel(mine_ref, theirs_ref, w_mine, w_theirs, out_ref):
    out = jnp.dot(mine_ref[...], w_mine[...], preferred_element_type=F32)
    out = out + jnp.dot(theirs_ref[...], w_theirs[...], preferred_element_type=F32)
    out_ref[...] = out.astype(out_ref.dtype)


def out_project(which, mine, theirs, w_mine, w_theirs, dtype):
    rows, depth = mine.shape[0] // 2, mine.shape[1]
    width = w_mine.shape[1]
    tile = width // 4
    ctx = pl.BlockSpec((rows, depth), lambda n: (which, 0))
    weight = pl.BlockSpec((depth, tile), lambda n: (0, n))
    return pl.pallas_call(
        out_project_kernel,
        grid=(width // tile,),
        out_shape=jax.ShapeDtypeStruct((rows, width), dtype),
        in_specs=[ctx, ctx, weight, weight],
        out_specs=pl.BlockSpec((rows, tile), lambda n: (0, n)),
        compiler_params=params(16),
        cost_estimate=cost(4 * rows * depth * width, 4 * w_mine.size),
        name="out_project",
    )(mine, theirs, w_mine, w_theirs)


def dispatch_kernel(own_ref, mixed_ref, far_ref, gain_ref, pick_ref, resid_ref, ffn_ref, *outs):
    resid = own_ref[...].astype(F32) + mixed_ref[...] + far_ref[...].astype(F32)
    resid = resid.astype(BF16)
    resid_ref[...] = resid
    ffn_in = rms_norm(resid, gain_ref[...])
    ffn_ref[...] = ffn_in
    rows = outs[0].shape[0]
    picked = jnp.dot(pick_ref[...], ffn_in, preferred_element_type=F32).astype(BF16)
    for s, out in enumerate(outs):
        out[...] = picked[s * rows : (s + 1) * rows]


def dispatch(own, mixed, far, gain, pick, count):
    rows, width = own.shape
    capacity = pick.shape[0] // count
    block = jax.ShapeDtypeStruct((rows, width), BF16)
    sent = jax.ShapeDtypeStruct((capacity, width), BF16)
    return pl.pallas_call(
        dispatch_kernel,
        out_shape=(block, block) + (sent,) * count,
        compiler_params=params(40),
        cost_estimate=cost(2 * pick.size * width, 4 * own.size + 2 * pick.shape[0] * width),
        name="dispatch",
    )(own, mixed, far, gain, pick)


def expert_kernel(*refs, count):
    ins, (gate_ref, up_ref, down_ref) = refs[:count], refs[count : count + 3]
    outs, (rows, total) = refs[count + 3 : 2 * count + 3], refs[2 * count + 3 :]
    size = ins[0].shape[0]
    step = pl.program_id(0)

    @pl.when(step == 0)
    def _():
        for s, ref in enumerate(ins):
            rows[s * size : (s + 1) * size] = ref[...]

    gate = jnp.dot(rows[...], gate_ref[0], preferred_element_type=F32)
    up = jnp.dot(rows[...], up_ref[0], preferred_element_type=F32)
    hidden = (jax.nn.silu(gate) * up).astype(BF16)
    part = jnp.dot(hidden, down_ref[0], preferred_element_type=F32)

    @pl.when(step == 0)
    def _():
        total[...] = part

    @pl.when(step > 0)
    def _():
        total[...] += part

    @pl.when(step == pl.num_programs(0) - 1)
    def _():
        for s, out in enumerate(outs):
            out[...] = total[s * size : (s + 1) * size].astype(BF16)


def expert(blocks, w_gate_up, w_down):
    count = len(blocks)
    size, width = blocks[0].shape
    ff = w_down.shape[1]
    tile = 256
    steps = ff // tile
    return pl.pallas_call(
        functools.partial(expert_kernel, count=count),
        grid=(steps,),
        out_shape=(jax.ShapeDtypeStruct((size, width), BF16),) * count,
        in_specs=[whole((size, width))] * count
        + [
            pl.BlockSpec((1, width, tile), lambda n: (0, 0, n)),
            pl.BlockSpec((1, width, tile), lambda n: (0, 0, n + steps)),
            pl.BlockSpec((1, tile, width), lambda n: (0, n, 0)),
        ],
        out_specs=(whole((size, width)),) * count,
        scratch_shapes=[
            pltpu.VMEM((count * size, width), BF16),
            pltpu.VMEM((count * size, width), F32),
        ],
        compiler_params=params(48),
        cost_estimate=cost(6 * count * size * width * ff, 6 * width * ff),
        name="expert",
    )(*blocks, w_gate_up, w_gate_up, w_down)


def combine_kernel(base_ref, weigh_ref, *refs):
    ins, out_ref, rows = refs[:-2], refs[-2], refs[-1]
    size = ins[0].shape[0]
    for s, ref in enumerate(ins):
        rows[s * size : (s + 1) * size] = ref[...]
    total = jnp.dot(weigh_ref[...], rows[...], preferred_element_type=F32)
    out_ref[...] = (base_ref[...].astype(F32) + total).astype(out_ref.dtype)


def combine(base, weigh, blocks, dtype):
    size, width = blocks[0].shape
    return pl.pallas_call(
        combine_kernel,
        out_shape=jax.ShapeDtypeStruct(base.shape, dtype),
        scratch_shapes=[pltpu.VMEM((len(blocks) * size, width), BF16)],
        compiler_params=params(32),
        cost_estimate=cost(2 * weigh.size * width, 2 * len(blocks) * size * width),
        name="combine",
    )(base, weigh, *blocks)


def on_device(
    residual_in,
    segment_ids,
    attn_gain,
    w_qkv,
    w_out,
    ffn_gain,
    w_router,
    routes,
    w_gate_up,
    w_down,
    page_owner,
):
    own = residual_in[0]
    tok_dev, width = own.shape
    heads_here = w_qkv.shape[1]
    head_dim = w_out.shape[1]
    seq_count = lax.axis_size("seq")
    blk_count = lax.axis_size("blk")
    group_len = seq_count * tok_dev
    seq_me = lax.axis_index("seq")
    blk_me = lax.axis_index("blk")
    seq_steps = jnp.arange(seq_count, dtype=jnp.int32)
    blk_steps = jnp.arange(blk_count, dtype=jnp.int32)

    far = swap(own, "seq", 2)
    core = swap(own, "seq", 1)
    far_core = swap(far, "seq", 1)
    w_mine = w_out.reshape(heads_here * head_dim, width)
    w_theirs = swap(w_mine, "seq", 1)

    capacity = tok_dev * 3 // 8
    route_rows = routes[0]
    experts = blk_me ^ blk_steps
    chosen = jnp.any(route_rows[:, :, None] == experts[None, None, :], axis=1)
    rank = jnp.cumsum(chosen.astype(jnp.int32), axis=0) - 1
    slot = jnp.where(chosen, rank, -1)
    slots = jnp.arange(capacity, dtype=jnp.int32)
    hit = slot.T[:, None, :] == slots[None, :, None]
    pick = hit.astype(BF16).reshape(blk_count * capacity, tok_dev)

    segment_blocks = segment_ids[0].reshape(seq_count, tok_dev)
    at = (seq_me ^ seq_steps)[:, None] == seq_steps[None, :]
    segment_row = jnp.sum(
        jnp.where(at[:, :, None], segment_blocks[None], 0), axis=1
    ).reshape(group_len)

    w_flat = w_qkv.reshape(width, heads_here * 3 * head_dim)
    gain = attn_gain[None]
    q_near, kv_near = project(own, core, gain, w_flat, heads_here, head_dim)
    q_far, kv_far = project(far, far_core, gain, w_flat, heads_here, head_dim)

    page_len = group_len // blk_count
    per_dev = tok_dev // page_len
    owners = page_owner[0]
    page_of = jnp.sum(
        jnp.where(owners[None, :] == experts[:, None], blk_steps[None, :], 0), axis=1
    )
    place = ((page_of // per_dev) ^ seq_me) * per_dev + page_of % per_dev
    outgoing = pages_out(place, kv_near, kv_far, blk_count)
    arrived = [outgoing[0]] + [swap(outgoing[s], "blk", s) for s in range(1, blk_count)]
    kv_cache = pages_in(experts, arrived)

    keep, send = attend(segment_row, q_near, q_far, kv_near, kv_far, head_dim)
    theirs = swap(send, "seq", 1)
    far_sum = out_project(1, keep, theirs, w_mine, w_theirs, BF16)
    from_far = swap(far_sum, "seq", 2)
    mixed = out_project(0, keep, theirs, w_mine, w_theirs, F32)

    resid, ffn_in, *sent = dispatch(own, mixed, from_far, ffn_gain[None], pick, blk_count)

    gates = jax.nn.sigmoid(jnp.dot(ffn_in, w_router, preferred_element_type=F32)).astype(BF16)
    expert_ids = jnp.arange(w_router.shape[1], dtype=jnp.int32)
    gate_of = jnp.sum(
        jnp.where(experts[:, None, None] == expert_ids[None, None, :], gates[None], 0), axis=2
    ).astype(BF16)
    weigh = jnp.where(hit, gate_of[:, None, :], 0).astype(BF16)
    weigh = weigh.reshape(blk_count * capacity, tok_dev).T

    half, quarter = blk_count // 2, blk_count // 4
    groups = [range(half), range(half, half + quarter), range(half + quarter, blk_count)]
    base = resid
    for number, group in enumerate(groups):
        blocks = [sent[s] if s == 0 else swap(sent[s], "blk", s) for s in group]
        outs = expert(blocks, w_gate_up, w_down)
        back = [out if s == 0 else swap(out, "blk", s) for s, out in zip(group, outs)]
        columns = weigh[:, group[0] * capacity : (group[-1] + 1) * capacity]
        base = combine(base, columns, back, BF16 if number == len(groups) - 1 else F32)
    return (base[None], kv_cache)


def solution(mesh):
    in_specs = (
        P("blk", "seq", None),
        P("blk", None),
        P(),
        P(None, "seq", None),
        P("seq", None, None),
        P(),
        P(),
        P("blk", "seq", None),
        P("blk", None, None),
        P("blk", None, None),
        P("blk", None),
    )
    out_specs = (P("blk", "seq", None), P("blk", None, None, "seq"))
    return jax.shard_map(
        on_device, mesh=mesh, in_specs=in_specs, out_specs=out_specs, check_vma=False
    )
```

```python
import functools
import math

import jax
import jax.numpy as jnp
from jax import lax
from jax.experimental import pallas as pl
from jax.experimental.pallas import tpu as pltpu
from jax.sharding import PartitionSpec as P

EPS = 1e-06
F32 = jnp.float32
BF16 = jnp.bfloat16
VMEM_SPEC = pl.BlockSpec(memory_space=pltpu.VMEM)
SMEM_SPEC = pl.BlockSpec(memory_space=pltpu.SMEM)


def rms_norm(value, gain):
    wide = value.astype(F32)
    scale = lax.rsqrt(jnp.mean(wide * wide, axis=-1, keepdims=True) + EPS)
    return (wide * scale * gain.astype(F32)).astype(BF16)


def swap(value, axis, step):
    size = lax.axis_size(axis)
    return lax.ppermute(value, axis, [(i, i ^ step) for i in range(size)])


def held(value):
    return pltpu.with_memory_space_constraint(value, pltpu.VMEM)


def array(shape, dtype=BF16):
    return jax.ShapeDtypeStruct(shape, dtype)


def call(kernel, name, out_shape, args, mib, flops, scratch=(), scalars=0):
    outs = out_shape if isinstance(out_shape, tuple) else (out_shape,)
    moved = sum(a.size * a.dtype.itemsize for a in (*args, *outs))
    return pl.pallas_call(
        kernel,
        out_shape=out_shape,
        in_specs=[SMEM_SPEC] * scalars + [VMEM_SPEC] * (len(args) - scalars),
        scratch_shapes=scratch,
        compiler_params=pltpu.CompilerParams(vmem_limit_bytes=mib << 20),
        cost_estimate=pl.CostEstimate(flops=flops, bytes_accessed=moved, transcendentals=0),
        name=name,
    )(*args)


def plan_kernel(routes_ref, pick_ref, *, count):
    top, rows = routes_ref.shape
    capacity = pick_ref.shape[0] // count
    expert = lax.axis_index("blk") ^ lax.broadcasted_iota(jnp.int32, (count, rows), 0)
    chosen = jnp.zeros((count, rows), F32)
    for t in range(top):
        chosen = jnp.maximum(chosen, jnp.where(routes_ref[t : t + 1] == expert, F32(1), F32(0)))
    before = lax.broadcasted_iota(jnp.int32, (rows, rows), 0)
    after = lax.broadcasted_iota(jnp.int32, (rows, rows), 1)
    upto = jnp.where(before <= after, F32(1), F32(0)).astype(BF16)
    rank = jnp.dot(chosen.astype(BF16), upto, preferred_element_type=F32) - 1
    slot = jnp.where(chosen > 0, rank, F32(-1))
    place = lax.broadcasted_iota(jnp.int32, (capacity, rows), 0).astype(F32)
    for s in range(count):
        hit = jnp.where(slot[s : s + 1] == place, F32(1), F32(0))
        pick_ref[s * capacity : (s + 1) * capacity] = hit.astype(BF16)


def plan(routes, count):
    top, rows = routes.shape
    capacity = rows * 3 // 8
    return call(
        functools.partial(plan_kernel, count=count),
        "plan",
        array((count * capacity, rows)),
        (routes,),
        4,
        2 * count * rows * rows,
    )


def project_rows(a_ref, b_ref, gain_ref, w_ref, q_ref, kv_ref, normed, head_dim):
    rows = a_ref.shape[0]
    normed[:rows] = rms_norm(a_ref[...], gain_ref[0:1])
    normed[rows:] = rms_norm(b_ref[...], gain_ref[0:1])
    for h in range(q_ref.shape[1] // head_dim):
        columns = slice(3 * h * head_dim, 3 * (h + 1) * head_dim)
        out = jnp.dot(normed[...], w_ref[:, columns], preferred_element_type=F32).astype(BF16)
        q_ref[:, h * head_dim : (h + 1) * head_dim] = out[:, :head_dim]
        kv_ref[:, 2 * h * head_dim : 2 * (h + 1) * head_dim] = out[:, head_dim:]


def project_kernel(a_ref, b_ref, gain_ref, w_ref, q_ref, kv_ref, normed, *, head_dim):
    project_rows(a_ref, b_ref, gain_ref, w_ref, q_ref, kv_ref, normed, head_dim)


def project(a, b, gains, w_flat, heads, head_dim):
    rows, width = a.shape
    return call(
        functools.partial(project_kernel, head_dim=head_dim),
        "project",
        (array((2 * rows, heads * head_dim)), array((2 * rows, heads * 2 * head_dim))),
        (a, b, gains, w_flat),
        12,
        4 * rows * w_flat.size,
        [pltpu.VMEM((2 * rows, width), BF16)],
    )


def attend_kernel(
    seg_ref,
    q_near,
    kv_near,
    a_ref,
    b_ref,
    gain_ref,
    w_ref,
    keep_ref,
    send_ref,
    q_far,
    kv_far,
    normed,
    bias,
    *,
    head_dim,
):
    project_rows(a_ref, b_ref, gain_ref, w_ref, q_far, kv_far, normed, head_dim)
    block = a_ref.shape[0]
    half = 2 * block
    me = lax.axis_index("seq")
    row = jnp.concatenate(
        [
            seg_ref[:, pl.ds(pl.multiple_of((me ^ k) * block, block), block)]
            for k in range(seg_ref.shape[1] // block)
        ],
        axis=1,
    ).astype(F32)
    column = jnp.broadcast_to(row, (8, row.shape[1])).T[:, 0:1]
    bias[...] = jnp.where(column == row, F32(0), F32(-1e30))
    factor = math.log2(math.e) / math.sqrt(head_dim)
    for h in range(q_near.shape[1] // head_dim):
        q_cols = slice(h * head_dim, (h + 1) * head_dim)
        k_cols = slice(2 * h * head_dim, (2 * h + 1) * head_dim)
        v_cols = slice((2 * h + 1) * head_dim, (2 * h + 2) * head_dim)
        key = jnp.concatenate([kv_near[:, k_cols], kv_far[:, k_cols]], axis=0)
        value = jnp.concatenate([kv_near[:, v_cols], kv_far[:, v_cols]], axis=0)
        for part, q_ref in enumerate((q_near, q_far)):
            scores = lax.dot_general(
                q_ref[:, q_cols], key, (((1,), (1,)), ((), ())), preferred_element_type=F32
            )
            scores = scores + bias[part * half : (part + 1) * half]
            top = jnp.max(scores, axis=-1, keepdims=True)
            weights = jnp.exp2((scores - top) * factor)
            total = jnp.sum(weights, axis=-1, keepdims=True)
            context = jnp.dot(weights.astype(BF16), value, preferred_element_type=F32)
            context = (context / total).astype(BF16)
            rows = slice(part * block, (part + 1) * block)
            keep_ref[rows, q_cols] = context[:block]
            send_ref[rows, q_cols] = context[block:]


def attend(segments, q_near, kv_near, a, b, gains, w_flat, head_dim):
    group_len = segments.shape[1]
    half, cols = q_near.shape
    return call(
        functools.partial(attend_kernel, head_dim=head_dim),
        "attend",
        (array((half, cols)), array((half, cols))),
        (segments, q_near, kv_near, a, b, gains, w_flat),
        16,
        2 * half * w_flat.size + 4 * group_len * group_len * cols,
        [
            pltpu.VMEM((half, cols), BF16),
            pltpu.VMEM((half, 2 * cols), BF16),
            pltpu.VMEM((half, a.shape[1]), BF16),
            pltpu.VMEM((group_len, group_len), F32),
        ],
    )


def out_project_kernel(mine_ref, theirs_ref, w_mine, w_theirs, out_ref, *, which):
    rows = slice(which * out_ref.shape[0], (which + 1) * out_ref.shape[0])
    out = jnp.dot(mine_ref[rows], w_mine[...], preferred_element_type=F32)
    out = out + jnp.dot(theirs_ref[rows], w_theirs[...], preferred_element_type=F32)
    out_ref[...] = out.astype(out_ref.dtype)


def out_project(which, mine, theirs, w_mine, w_theirs, dtype):
    rows, depth = mine.shape[0] // 2, mine.shape[1]
    width = w_mine.shape[1]
    return call(
        functools.partial(out_project_kernel, which=which),
        "out_project",
        array((rows, width), dtype),
        (mine, theirs, w_mine, w_theirs),
        8,
        4 * rows * depth * width,
    )


def pages_out_kernel(owner_ref, *refs, count):
    blocks, outs, (rows, pages) = refs[:-count - 2], refs[-count - 2 : -2], refs[-2:]
    size = blocks[0].shape[0]
    page_len, share = outs[0].shape
    seq_me, blk_me = lax.axis_index("seq"), lax.axis_index("blk")
    columns = pl.ds(pl.multiple_of(seq_me * share, share), share)
    for k, block in enumerate(blocks):
        start = pl.multiple_of((seq_me ^ k) * size, size)
        rows[pl.ds(start, size)] = block[:, columns]
    for j in range(count):
        pages[owner_ref[0, j] ^ blk_me] = rows[j * page_len : (j + 1) * page_len]
    for s, out in enumerate(outs):
        out[...] = pages[s]


def pages_out(owners, blocks):
    count = owners.shape[1]
    group_len = len(blocks) * blocks[0].shape[0]
    page_len, share = group_len // count, blocks[0].shape[1] // len(blocks)
    return call(
        functools.partial(pages_out_kernel, count=count),
        "pages_out",
        (array((page_len, share)),) * count,
        (owners, *blocks),
        8,
        0,
        [pltpu.VMEM((group_len, share), BF16), pltpu.VMEM((count, page_len, share), BF16)],
        scalars=1,
    )


def pages_in_kernel(*refs):
    pages, out = refs[:-1], refs[-1]
    page_len = pages[0].shape[0]
    blk_me = lax.axis_index("blk")
    for s, page in enumerate(pages):
        out[pl.ds(pl.multiple_of((blk_me ^ s) * page_len, page_len), page_len)] = page[...]


def pages_in(pages):
    page_len, share = pages[0].shape
    return call(
        pages_in_kernel, "pages_in", array((len(pages) * page_len, share)), tuple(pages), 4, 0
    )


def cache_kernel(*refs, head_dim):
    *shares, gain_ref, w_ref, out_ref, rows = refs
    share = shares[0].shape[1]
    me = lax.axis_index("seq")
    for k, ref in enumerate(shares):
        rows[:, pl.ds(pl.multiple_of((me ^ k) * share, share), share)] = ref[...]
    rows[...] = rms_norm(rows[...], gain_ref[0:1])
    count, page_len = out_ref.shape[1:3]
    for h in range(out_ref.shape[3] // (2 * head_dim)):
        columns = slice((3 * h + 1) * head_dim, 3 * (h + 1) * head_dim)
        out = jnp.dot(rows[...], w_ref[:, columns], preferred_element_type=F32).astype(BF16)
        out = out.reshape(count, page_len, 2 * head_dim)
        out_ref[0, :, :, 2 * h * head_dim : 2 * (h + 1) * head_dim] = out


def cache(shares, gains, w_flat, count, heads, head_dim):
    group_len, share = shares[0].shape
    return call(
        functools.partial(cache_kernel, head_dim=head_dim),
        "cache",
        array((1, count, group_len // count, heads * 2 * head_dim)),
        (*shares, gains, w_flat),
        16,
        2 * group_len * w_flat.size,
        [pltpu.VMEM((group_len, share * len(shares)), BF16)],
    )


def dispatch_kernel(own_ref, mixed_ref, far_ref, gain_ref, pick_ref, resid_ref, ffn_ref, *outs):
    resid = own_ref[...].astype(F32) + mixed_ref[...] + far_ref[...].astype(F32)
    resid = resid.astype(BF16)
    resid_ref[...] = resid
    ffn_in = rms_norm(resid, gain_ref[1:2])
    ffn_ref[...] = ffn_in
    rows = outs[0].shape[0]
    picked = jnp.dot(pick_ref[...], ffn_in, preferred_element_type=F32).astype(BF16)
    for s, out in enumerate(outs):
        out[...] = picked[s * rows : (s + 1) * rows]


def dispatch(own, mixed, far, gains, pick, count):
    rows, width = own.shape
    capacity = pick.shape[0] // count
    return call(
        dispatch_kernel,
        "dispatch",
        (array((rows, width)),) * 2 + (array((capacity, width)),) * count,
        (own, mixed, far, gains, pick),
        max(12, pick.shape[0] * width * 12 >> 20),
        2 * pick.size * width,
    )


def weigh_kernel(ffn_ref, router_ref, pick_ref, *outs, capacity):
    logits = lax.dot_general(
        router_ref[...], ffn_ref[...], (((1,), (1,)), ((), ())), preferred_element_type=F32
    )
    gates = jax.nn.sigmoid(logits).astype(BF16)
    experts = gates.shape[0]
    step = lax.broadcasted_iota(jnp.int32, (experts, experts), 0)
    expert = lax.broadcasted_iota(jnp.int32, (experts, experts), 1)
    order = jnp.where(lax.axis_index("blk") ^ step == expert, F32(1), F32(0)).astype(BF16)
    gates = jnp.dot(order, gates, preferred_element_type=F32)
    start = 0
    for out in outs:
        parts = [
            pick_ref[s * capacity : (s + 1) * capacity].astype(F32) * gates[s : s + 1]
            for s in range(start, start + out.shape[1] // capacity)
        ]
        out[...] = jnp.concatenate(parts, axis=0).T.astype(BF16)
        start += out.shape[1] // capacity


def weigh(ffn_in, router, pick, groups):
    rows = ffn_in.shape[0]
    capacity = pick.shape[0] // router.shape[0]
    return call(
        functools.partial(weigh_kernel, capacity=capacity),
        "weigh",
        tuple(array((rows, len(group) * capacity)) for group in groups),
        (ffn_in, router, pick),
        8,
        2 * router.size * rows,
    )


def expert_kernel(*refs, count):
    ins, (in_ref, down_ref) = refs[:count], refs[count : count + 2]
    outs, (rows, hidden) = refs[count + 2 : 2 * count + 2], refs[2 * count + 2 :]
    size = ins[0].shape[0]
    ff, width = down_ref.shape
    for s, ref in enumerate(ins):
        rows[s * size : (s + 1) * size] = ref[...]
    tile = min(ff, 512)
    for start in range(0, ff, tile):
        gate = jnp.dot(rows[...], in_ref[:, start : start + tile], preferred_element_type=F32)
        up = jnp.dot(
            rows[...], in_ref[:, ff + start : ff + start + tile], preferred_element_type=F32
        )
        hidden[:, start : start + tile] = (jax.nn.silu(gate) * up).astype(BF16)
    for start in range(0, width, tile):
        part = jnp.dot(hidden[...], down_ref[:, start : start + tile], preferred_element_type=F32)
        for s, out in enumerate(outs):
            out[:, start : start + tile] = part[s * size : (s + 1) * size].astype(BF16)


def expert(blocks, gate_up, down):
    count = len(blocks)
    size, width = blocks[0].shape
    ff = down.shape[0]
    return call(
        functools.partial(expert_kernel, count=count),
        "expert",
        (array((size, width)),) * count,
        (*blocks, gate_up, down),
        max(8, count * size * 20480 >> 20),
        6 * count * size * width * ff,
        [
            pltpu.VMEM((count * size, width), BF16),
            pltpu.VMEM((count * size, ff), BF16),
        ],
    )


def combine_kernel(base_ref, weigh_ref, *refs):
    ins, out_ref, rows = refs[:-2], refs[-2], refs[-1]
    size = ins[0].shape[0]
    for s, ref in enumerate(ins):
        rows[s * size : (s + 1) * size] = ref[...]
    total = jnp.dot(weigh_ref[...], rows[...], preferred_element_type=F32)
    out_ref[...] = (base_ref[...].astype(F32) + total).astype(out_ref.dtype)


def combine(base, weights, blocks, dtype):
    size, width = blocks[0].shape
    return call(
        combine_kernel,
        "combine",
        array(base.shape, dtype),
        (base, weights, *blocks),
        8,
        2 * weights.size * width,
        [pltpu.VMEM((len(blocks) * size, width), BF16)],
    )


def on_device(
    residual_in,
    segment_ids,
    attn_gain,
    w_qkv,
    w_out,
    ffn_gain,
    w_router,
    routes,
    w_gate_up,
    w_down,
    page_owner,
):
    own = residual_in[0]
    width = own.shape[1]
    heads_here = w_qkv.shape[1]
    head_dim = w_out.shape[1]
    blk_count = lax.axis_size("blk")

    far = swap(own, "seq", 2)
    core = swap(own, "seq", 1)
    w_mine = w_out.reshape(heads_here * head_dim, width)
    w_theirs = swap(w_mine, "seq", 1)
    gains = jnp.stack([attn_gain, ffn_gain])
    pick = plan(routes[0].T, blk_count)

    w_flat = held(w_qkv.reshape(width, heads_here * 3 * head_dim))
    q_near, kv_near = project(own, core, gains, w_flat, heads_here, head_dim)
    far, q_near, kv_near = lax.optimization_barrier((far, q_near, kv_near))
    far_core = swap(far, "seq", 1)
    keep, send = attend(segment_ids, q_near, kv_near, far, far_core, gains, w_flat, head_dim)
    theirs = swap(send, "seq", 1)
    w_mine, w_theirs = held(w_mine), held(w_theirs)
    far_sum = out_project(1, keep, theirs, w_mine, w_theirs, BF16)
    from_far = swap(far_sum, "seq", 2)
    mixed = out_project(0, keep, theirs, w_mine, w_theirs, F32)

    outgoing = pages_out(page_owner, (own, core, far, far_core))
    arrived = [outgoing[0]] + [swap(outgoing[s], "blk", s) for s in range(1, blk_count)]
    share = pages_in(arrived)
    share_far, share_core = swap(share, "seq", 2), swap(share, "seq", 1)
    share_far_core = swap(share_far, "seq", 1)
    kv_cache = cache(
        (share, share_core, share_far, share_far_core),
        gains,
        w_flat,
        blk_count,
        heads_here,
        head_dim,
    )

    resid, ffn_in, *sent = dispatch(own, mixed, from_far, gains, pick, blk_count)
    half, quarter = blk_count // 2, blk_count // 4
    groups = [range(half), range(half, half + quarter), range(half + quarter, blk_count)]
    weights = weigh(ffn_in, w_router.T, pick, groups)
    gate_up, down = held(w_gate_up[0]), held(w_down[0])
    total = resid
    for number, group in enumerate(groups):
        blocks = [sent[s] if s == 0 else swap(sent[s], "blk", s) for s in group]
        outs = expert(blocks, gate_up, down)
        back = [out if s == 0 else swap(out, "blk", s) for s, out in zip(group, outs)]
        last = number == len(groups) - 1
        total = combine(total, weights[number], back, BF16 if last else F32)
    return (total[None], kv_cache)


def solution(mesh):
    in_specs = (
        P("blk", "seq", None),
        P("blk", None),
        P(),
        P(None, "seq", None),
        P("seq", None, None),
        P(),
        P(),
        P("blk", "seq", None),
        P("blk", None, None),
        P("blk", None, None),
        P("blk", None),
    )
    out_specs = (P("blk", "seq", None), P("blk", None, None, "seq"))
    return jax.shard_map(
        on_device, mesh=mesh, in_specs=in_specs, out_specs=out_specs, check_vma=False
    )
```

```python
import functools
import math

import jax
import jax.numpy as jnp
from jax import lax
from jax.experimental import pallas as pl
from jax.experimental.pallas import tpu as pltpu
from jax.sharding import PartitionSpec as P

EPS = 1e-06
F32 = jnp.float32
BF16 = jnp.bfloat16
VMEM_SPEC = pl.BlockSpec(memory_space=pltpu.VMEM)
SMEM_SPEC = pl.BlockSpec(memory_space=pltpu.SMEM)


def rms_norm(value, gain):
    wide = value.astype(F32)
    scale = lax.rsqrt(jnp.mean(wide * wide, axis=-1, keepdims=True) + EPS)
    return (wide * scale * gain.astype(F32)).astype(BF16)


def swap(value, axis, step):
    size = lax.axis_size(axis)
    return lax.ppermute(value, axis, [(i, i ^ step) for i in range(size)])


def held(value):
    return pltpu.with_memory_space_constraint(value, pltpu.VMEM)


def array(shape, dtype=BF16):
    return jax.ShapeDtypeStruct(shape, dtype)


def call(kernel, name, out_shape, args, mib, flops, scratch=(), scalars=0):
    return pl.pallas_call(
        kernel,
        out_shape=out_shape,
        in_specs=[SMEM_SPEC] * scalars + [VMEM_SPEC] * (len(args) - scalars),
        scratch_shapes=scratch,
        compiler_params=pltpu.CompilerParams(vmem_limit_bytes=mib << 20),
        cost_estimate=pl.CostEstimate(flops=flops, bytes_accessed=0, transcendentals=0),
        name=name,
    )(*args)


def plan_kernel(routes_ref, *outs, groups):
    top, rows = routes_ref.shape
    count = sum(map(len, groups))
    capacity = outs[0].shape[0] // len(groups[0])
    expert = lax.axis_index("blk") ^ lax.broadcasted_iota(jnp.int32, (count, rows), 0)
    chosen = jnp.zeros((count, rows), F32)
    for t in range(top):
        chosen = jnp.maximum(chosen, jnp.where(routes_ref[t : t + 1] == expert, F32(1), F32(0)))
    before = lax.broadcasted_iota(jnp.int32, (rows, rows), 0)
    after = lax.broadcasted_iota(jnp.int32, (rows, rows), 1)
    upto = jnp.where(before <= after, F32(1), F32(0)).astype(BF16)
    rank = jnp.dot(chosen.astype(BF16), upto, preferred_element_type=F32) - 1
    slot = jnp.where(chosen > 0, rank, F32(-1))
    place = lax.broadcasted_iota(jnp.int32, (capacity, rows), 0).astype(F32)
    for group, out in zip(groups, outs):
        for i, s in enumerate(group):
            hit = jnp.where(slot[s : s + 1] == place, F32(1), F32(0))
            out[i * capacity : (i + 1) * capacity] = hit.astype(BF16)


def plan(routes, groups):
    top, rows = routes.shape
    capacity = rows * 3 // 8
    return call(
        functools.partial(plan_kernel, groups=groups),
        "plan",
        tuple(array((len(group) * capacity, rows)) for group in groups),
        (routes,),
        4,
        0,
    )


def project_rows(blocks, gain_ref, w_ref, q_ref, kv_ref, normed, head_dim):
    rows = blocks[0].shape[0]
    for i, block in enumerate(blocks):
        normed[i * rows : (i + 1) * rows] = rms_norm(block[...], gain_ref[0:1])
    for h in range(q_ref.shape[1] // head_dim):
        columns = slice(3 * h * head_dim, 3 * (h + 1) * head_dim)
        out = jnp.dot(normed[...], w_ref[:, columns], preferred_element_type=F32).astype(BF16)
        q_ref[:, h * head_dim : (h + 1) * head_dim] = out[:, :head_dim]
        kv_ref[:, 2 * h * head_dim : 2 * (h + 1) * head_dim] = out[:, head_dim:]


def project_kernel(*refs, head_dim):
    *blocks, gain_ref, w_ref, q_ref, kv_ref, normed = refs
    project_rows(blocks, gain_ref, w_ref, q_ref, kv_ref, normed, head_dim)


def project(blocks, gains, w_flat, heads, head_dim):
    rows, width = len(blocks) * blocks[0].shape[0], blocks[0].shape[1]
    return call(
        functools.partial(project_kernel, head_dim=head_dim),
        "project",
        (array((rows, heads * head_dim)), array((rows, heads * 2 * head_dim))),
        (*blocks, gains, w_flat),
        12,
        0,
        [pltpu.VMEM((rows, width), BF16)],
    )


def attend_rows(first, seg_ref, queries, kvs, keep_ref, send_ref, bias, head_dim):
    block = keep_ref.shape[0]
    me = lax.axis_index("seq")
    row = jnp.concatenate(
        [
            seg_ref[:, pl.ds(pl.multiple_of((me ^ k) * block, block), block)]
            for k in range(seg_ref.shape[1] // block)
        ],
        axis=1,
    ).astype(F32)
    column = jnp.broadcast_to(row, (8, row.shape[1])).T[first : first + 2 * block, 0:1]
    bias[...] = jnp.where(column == row, F32(0), F32(-1e30))
    factor = math.log2(math.e) / math.sqrt(head_dim)
    for h in range(queries[0].shape[1] // head_dim):
        q_cols = slice(h * head_dim, (h + 1) * head_dim)
        k_cols = slice(2 * h * head_dim, (2 * h + 1) * head_dim)
        v_cols = slice((2 * h + 1) * head_dim, (2 * h + 2) * head_dim)
        query = jnp.concatenate([ref[:, q_cols] for ref in queries], axis=0)
        key = jnp.concatenate([ref[:, k_cols] for ref in kvs], axis=0)
        value = jnp.concatenate([ref[:, v_cols] for ref in kvs], axis=0)
        scores = lax.dot_general(
            query, key, (((1,), (1,)), ((), ())), preferred_element_type=F32
        )
        scores = scores + bias[...]
        top = jnp.max(scores, axis=-1, keepdims=True)
        weights = jnp.exp2((scores - top) * factor)
        total = jnp.sum(weights, axis=-1, keepdims=True)
        context = jnp.dot(weights.astype(BF16), value, preferred_element_type=F32)
        context = (context / total).astype(BF16)
        keep_ref[:, q_cols] = context[:block]
        send_ref[:, q_cols] = context[block:]


def attend_near_kernel(seg, q, kv_near, kv_far, kv_last, keep, send, bias, *, head_dim):
    attend_rows(0, seg, [q], [kv_near, kv_far, kv_last], keep, send, bias, head_dim)


def attend_near(segments, q, kvs, head_dim):
    rows, cols = q.shape
    group_len = segments.shape[1]
    return call(
        functools.partial(attend_near_kernel, head_dim=head_dim),
        "attend_near",
        (array((rows // 2, cols)),) * 2,
        (segments, q, *kvs),
        12,
        1 << 34,
        [pltpu.VMEM((rows, group_len), F32)],
    )


def attend_far_kernel(
    seg, q_far, kv_near, kv_far, block, gain, w_ref, keep, send, kv, q, normed, bias, *, head_dim
):
    project_rows([block], gain, w_ref, q, kv, normed, head_dim)
    first = kv_near.shape[0]
    attend_rows(first, seg, [q_far, q], [kv_near, kv_far, kv], keep, send, bias, head_dim)


def attend_far(segments, q_far, kv_near, kv_far, block, gains, w_flat, head_dim):
    rows, cols = q_far.shape
    group_len = segments.shape[1]
    return call(
        functools.partial(attend_far_kernel, head_dim=head_dim),
        "attend_far",
        (array((rows, cols)),) * 2 + (array((rows, 2 * cols)),),
        (segments, q_far, kv_near, kv_far, block, gains, w_flat),
        12,
        0,
        [
            pltpu.VMEM((rows, cols), BF16),
            pltpu.VMEM(block.shape, BF16),
            pltpu.VMEM((2 * rows, group_len), F32),
        ],
    )


def out_project_kernel(mine_ref, theirs_ref, w_mine, w_theirs, out_ref):
    out = jnp.dot(mine_ref[...], w_mine[...], preferred_element_type=F32)
    out = out + jnp.dot(theirs_ref[...], w_theirs[...], preferred_element_type=F32)
    out_ref[...] = out.astype(out_ref.dtype)


def out_project(mine, theirs, w_mine, w_theirs, dtype):
    rows, depth = mine.shape
    width = w_mine.shape[1]
    return call(
        out_project_kernel,
        "out_project",
        array((rows, width), dtype),
        (mine, theirs, w_mine, w_theirs),
        8,
        0,
    )


def join_rows(refs, spans, out):
    at = 0
    for ref, (low, high) in zip(refs, spans):
        out[at : at + high - low] = ref[low:high]
        at += high - low


def join_kernel(*refs, spans):
    join_rows(refs[:-1], spans, refs[-1])


def split(parts):
    arrays = tuple(part[0] for part in parts)
    spans = tuple((low, high) for _, low, high in parts)
    return arrays, spans, sum(high - low for low, high in spans)


def full(value):
    return (value, 0, value.shape[0])


def join(parts):
    arrays, spans, rows = split(parts)
    return call(
        functools.partial(join_kernel, spans=spans),
        "join",
        array((rows, arrays[0].shape[1])),
        arrays,
        4,
        0,
    )


def pages_out_kernel(owner_ref, *refs, count):
    *blocks, rows, pages = refs
    blocks, outs = blocks[: -(count // 4)], blocks[-(count // 4) :]
    size = blocks[0].shape[0]
    page_len = outs[0].shape[0]
    seq_me, blk_me = lax.axis_index("seq"), lax.axis_index("blk")
    for k, block in enumerate(blocks):
        rows[pl.ds(pl.multiple_of((seq_me ^ k) * size, size), size)] = block[...]
    for j in range(count):
        step = owner_ref[0, j] ^ blk_me

        @pl.when(step % 4 == seq_me)
        def _(j=j, step=step):
            pages[step // 4] = rows[j * page_len : (j + 1) * page_len]

    for k, out in enumerate(outs):
        out[...] = pages[k]


def pages_out(owners, blocks):
    count = owners.shape[1]
    size, width = blocks[0].shape
    group_len = len(blocks) * size
    page_len = group_len // count
    return call(
        functools.partial(pages_out_kernel, count=count),
        "pages_out",
        (array((page_len, width)),) * (count // 4),
        (owners, *blocks),
        8,
        0,
        [pltpu.VMEM((group_len, width), BF16), pltpu.VMEM((count // 4, page_len, width), BF16)],
        scalars=1,
    )


def to_owner(page, number):
    seq_count, blk_count = lax.axis_size("seq"), lax.axis_size("blk")
    pairs = [
        (i * blk_count + b, i * blk_count + (b ^ (4 * number + i)))
        for i in range(seq_count)
        for b in range(blk_count)
    ]
    return lax.ppermute(page, ("seq", "blk"), pairs)


def cache_kernel(mine_ref, theirs_ref, gain_ref, w_ref, out_ref, rows, *, head_dim):
    count, page_len = out_ref.shape[1:3]
    seq_me, blk_me = lax.axis_index("seq"), lax.axis_index("blk")
    half = count // 4 * page_len
    for core, ref in enumerate((mine_ref, theirs_ref)):
        for chip in range(2):
            for k in range(count // 4):
                start = (blk_me ^ (4 * k + (seq_me ^ (2 * chip + core)))) * page_len
                page = ref[chip * half + k * page_len : chip * half + (k + 1) * page_len]
                rows[pl.ds(pl.multiple_of(start, page_len), page_len)] = page
    rows[...] = rms_norm(rows[...], gain_ref[0:1])
    for h in range(out_ref.shape[3] // (2 * head_dim)):
        columns = slice((3 * h + 1) * head_dim, 3 * (h + 1) * head_dim)
        out = jnp.dot(rows[...], w_ref[:, columns], preferred_element_type=F32).astype(BF16)
        out = out.reshape(count, page_len, 2 * head_dim)
        out_ref[0, :, :, 2 * h * head_dim : 2 * (h + 1) * head_dim] = out


def cache(mine, theirs, gains, w_flat, count, heads, head_dim):
    rows, width = mine.shape
    return call(
        functools.partial(cache_kernel, head_dim=head_dim),
        "cache",
        array((1, count, 2 * rows // count, heads * 2 * head_dim)),
        (mine, theirs, gains, w_flat),
        16,
        0,
        [pltpu.VMEM((2 * rows, width), BF16)],
    )


def pick_rows(pick, ffn_in, outs):
    picked = jnp.dot(pick, ffn_in, preferred_element_type=F32).astype(BF16)
    at = 0
    for out in outs:
        out[...] = picked[at : at + out.shape[0]]
        at += out.shape[0]


def dispatch_kernel(own_ref, mixed_ref, far_ref, gain_ref, pick_ref, resid_ref, ffn_ref, *outs):
    resid = own_ref[...].astype(F32) + mixed_ref[...] + far_ref[...].astype(F32)
    resid = resid.astype(BF16)
    resid_ref[...] = resid
    ffn_in = rms_norm(resid, gain_ref[1:2])
    ffn_ref[...] = ffn_in
    pick_rows(pick_ref[...], ffn_in, outs)


def dispatch(own, mixed, far, gains, pick, count):
    rows, width = own.shape
    capacity = pick.shape[0] // count
    return call(
        dispatch_kernel,
        "dispatch",
        (array((rows, width)),) * 2 + (array((capacity, width)),) * count,
        (own, mixed, far, gains, pick),
        max(10, pick.shape[0] * width * 12 >> 20),
        0,
    )


def dispatch_more_kernel(ffn_ref, pick_ref, *outs):
    pick_rows(pick_ref[...], ffn_ref[...], outs)


def dispatch_more(ffn_in, pick, sizes):
    width = ffn_in.shape[1]
    return call(
        dispatch_more_kernel,
        "dispatch_more",
        tuple(array((size, width)) for size in sizes),
        (ffn_in, pick),
        max(10, pick.shape[0] * width * 12 >> 20),
        1 << 34,
    )


def weigh_kernel(ffn_ref, router_ref, *refs, groups):
    logits = lax.dot_general(
        router_ref[...], ffn_ref[...], (((1,), (1,)), ((), ())), preferred_element_type=F32
    )
    gates = jax.nn.sigmoid(logits).astype(BF16)
    experts = gates.shape[0]
    step = lax.broadcasted_iota(jnp.int32, (experts, experts), 0)
    expert = lax.broadcasted_iota(jnp.int32, (experts, experts), 1)
    order = jnp.where(lax.axis_index("blk") ^ step == expert, F32(1), F32(0)).astype(BF16)
    gates = jnp.dot(order, gates, preferred_element_type=F32)
    for group, pick, out in zip(groups, refs[: len(groups)], refs[len(groups) :]):
        capacity = pick.shape[0] // len(group)
        parts = [
            pick[i * capacity : (i + 1) * capacity].astype(F32) * gates[s : s + 1]
            for i, s in enumerate(group)
        ]
        out[...] = jnp.concatenate(parts, axis=0).T.astype(BF16)


def weigh(ffn_in, router, picks, groups):
    return call(
        functools.partial(weigh_kernel, groups=groups),
        "weigh",
        tuple(array(pick.shape[::-1]) for pick in picks),
        (ffn_in, router, *picks),
        8,
        0,
    )


def expert_kernel(*refs, spans):
    count = len(spans)
    in_ref, down_ref = refs[count : count + 2]
    *outs, rows, hidden = refs[count + 2 :]
    ff, width = down_ref.shape
    join_rows(refs[:count], spans, rows)
    tile = min(ff, 512)
    for start in range(0, ff, tile):
        gate = jnp.dot(rows[...], in_ref[:, start : start + tile], preferred_element_type=F32)
        up = jnp.dot(
            rows[...], in_ref[:, ff + start : ff + start + tile], preferred_element_type=F32
        )
        hidden[:, start : start + tile] = (jax.nn.silu(gate) * up).astype(BF16)
    for start in range(0, width, tile):
        part = jnp.dot(hidden[...], down_ref[:, start : start + tile], preferred_element_type=F32)
        at = 0
        for out in outs:
            out[:, start : start + tile] = part[at : at + out.shape[0]].astype(BF16)
            at += out.shape[0]


def expert(parts, gate_up, down):
    arrays, spans, rows = split(parts)
    ff, width = down.shape
    return call(
        functools.partial(expert_kernel, spans=spans),
        "expert",
        tuple(array((high - low, width)) for low, high in spans),
        (*arrays, gate_up, down),
        max(8, rows * 20480 >> 20),
        1 << 35,
        [pltpu.VMEM((rows, width), BF16), pltpu.VMEM((rows, ff), BF16)],
    )


def combine_kernel(base_ref, weigh_ref, *refs, spans):
    *ins, out_ref, rows = refs
    join_rows(ins, spans, rows)
    total = jnp.dot(weigh_ref[...], rows[...], preferred_element_type=F32)
    out_ref[...] = (base_ref[...].astype(F32) + total).astype(out_ref.dtype)


def combine(base, weights, parts, dtype):
    arrays, spans, rows = split(parts)
    return call(
        functools.partial(combine_kernel, spans=spans),
        "combine",
        array(base.shape, dtype),
        (base, weights, *arrays),
        max(8, rows * 16384 >> 20),
        0,
        [pltpu.VMEM((rows, base.shape[1]), BF16)],
    )


def on_device(
    residual_in,
    segment_ids,
    attn_gain,
    w_qkv,
    w_out,
    ffn_gain,
    w_router,
    routes,
    w_gate_up,
    w_down,
    page_owner,
):
    own = residual_in[0]
    width = own.shape[1]
    heads_here = w_qkv.shape[1]
    head_dim = w_out.shape[1]
    blk_count = lax.axis_size("blk")

    slots = own.shape[0] * 3 // 8
    half = (4 + blk_count) // 2
    near, first, last = tuple(range(4)), tuple(range(4, half)), tuple(range(half, blk_count))
    groups = (first, (*near, *last))
    picks = plan(routes[0].T, groups)

    far = swap(own, "seq", 2)
    w_mine = w_out.reshape(heads_here * head_dim, width)
    picks, w_mine, to_core = lax.optimization_barrier((picks, w_mine, own))
    core = swap(to_core, "seq", 1)
    w_theirs = swap(w_mine, "seq", 1)
    gains = jnp.stack([attn_gain, ffn_gain])

    w_flat = held(w_qkv.reshape(width, heads_here * 3 * head_dim))
    q_near, kv_near = project((own, core), gains, w_flat, heads_here, head_dim)
    far, q_near, kv_near = lax.optimization_barrier((far, q_near, kv_near))
    far_core = swap(far, "seq", 1)
    q_far, kv_far = project((far,), gains, w_flat, heads_here, head_dim)
    keep_far, send_far, kv_last = attend_far(
        segment_ids, q_far, kv_near, kv_far, far_core, gains, w_flat, head_dim
    )
    w_mine, w_theirs = held(w_mine), held(w_theirs)
    theirs_far = swap(send_far, "seq", 1)
    outgoing = pages_out(page_owner, (own, core, far, far_core))
    theirs_far, outgoing = lax.optimization_barrier((theirs_far, outgoing))
    far_sum = out_project(keep_far, theirs_far, w_mine, w_theirs, BF16)
    far_sum, outgoing = lax.optimization_barrier((far_sum, outgoing))
    from_far = swap(far_sum, "seq", 2)
    arrived = [to_owner(page, k) for k, page in enumerate(outgoing)]
    keep, send = attend_near(segment_ids, q_near, (kv_near, kv_far, kv_last), head_dim)
    mixed = out_project(keep, swap(send, "seq", 1), w_mine, w_theirs, F32)

    gate_up, down = held(w_gate_up[0]), held(w_down[0])

    def there(group, blocks):
        pairs = zip(group, blocks)
        return tuple(swap(block, "blk", step) if step else block for step, block in pairs)

    def work(blocks):
        return expert([full(block) for block in blocks], gate_up, down)

    from_far, arrived = lax.optimization_barrier((from_far, arrived))
    resid, ffn_in, *sent_first = dispatch(own, mixed, from_far, gains, picks[0], len(first))
    rows_first = there(first, sent_first)
    sent = dispatch_more(ffn_in, picks[1], (slots,) * len(groups[1]))
    sent_near, sent_last = sent[: len(near)], sent[len(near) :]
    rows_near = there(near, sent_near)
    share = join([full(page) for page in arrived])
    share_far = swap(share, "seq", 2)
    rows_last = there(last, sent_last)
    first_out = work(rows_first)
    back_first = there(first, first_out)
    rows_near, first_out, share_far = lax.optimization_barrier((rows_near, first_out, share_far))
    both = join([full(share), full(share_far)])
    both_core = swap(both, "seq", 1)
    near_out = work(rows_near)
    rows_last, both_core = lax.optimization_barrier((rows_last, both_core))
    last_out = work(rows_last)
    back_last = there(last, last_out)
    near_out, last_out, both_core = lax.optimization_barrier((near_out, last_out, both_core))
    back_near = there(near, near_out)
    kv_cache = cache(both, both_core, gains, w_flat, blk_count, heads_here, head_dim)

    weights = weigh(ffn_in, w_router.T, picks, groups)
    total = combine(resid, weights[0], [full(block) for block in back_first], F32)
    kv_cache, total = lax.optimization_barrier((kv_cache, total))
    parts = [full(block) for block in (*back_near, *back_last)]
    total = combine(total, weights[1], parts, BF16)
    return (total[None], kv_cache)


def solution(mesh):
    in_specs = (
        P("blk", "seq", None),
        P("blk", None),
        P(),
        P(None, "seq", None),
        P("seq", None, None),
        P(),
        P(),
        P("blk", "seq", None),
        P("blk", None, None),
        P("blk", None, None),
        P("blk", None),
    )
    out_specs = (P("blk", "seq", None), P("blk", None, None, "seq"))
    return jax.shard_map(
        on_device, mesh=mesh, in_specs=in_specs, out_specs=out_specs, check_vma=False
    )
```

```python
import functools
import math

import jax
import jax.numpy as jnp
from jax import lax
from jax.experimental import pallas as pl
from jax.experimental.pallas import tpu as pltpu
from jax.sharding import PartitionSpec as P

EPS = 1e-06
F32 = jnp.float32
BF16 = jnp.bfloat16
VMEM_SPEC = pl.BlockSpec(memory_space=pltpu.VMEM)
SMEM_SPEC = pl.BlockSpec(memory_space=pltpu.SMEM)


def rms_norm(value, gain):
    wide = value.astype(F32)
    scale = lax.rsqrt(jnp.mean(wide * wide, axis=-1, keepdims=True) + EPS)
    return (wide * scale * gain.astype(F32)).astype(BF16)


def swap(value, axis, step):
    size = lax.axis_size(axis)
    return lax.ppermute(value, axis, [(i, i ^ step) for i in range(size)])


def held(value):
    return pltpu.with_memory_space_constraint(value, pltpu.VMEM)


def array(shape, dtype=BF16):
    return jax.ShapeDtypeStruct(shape, dtype)


def call(kernel, name, out_shape, args, mib, flops, scratch=(), scalars=0):
    return pl.pallas_call(
        kernel,
        out_shape=out_shape,
        in_specs=[SMEM_SPEC] * scalars + [VMEM_SPEC] * (len(args) - scalars),
        scratch_shapes=scratch,
        compiler_params=pltpu.CompilerParams(vmem_limit_bytes=mib << 20),
        cost_estimate=pl.CostEstimate(flops=flops, bytes_accessed=0, transcendentals=0),
        name=name,
    )(*args)


def plan_kernel(routes_ref, *outs, groups):
    top, rows = routes_ref.shape
    count = sum(map(len, groups))
    capacity = outs[0].shape[0] // len(groups[0])
    expert = lax.axis_index("blk") ^ lax.broadcasted_iota(jnp.int32, (count, rows), 0)
    chosen = jnp.zeros((count, rows), F32)
    for t in range(top):
        chosen = jnp.maximum(chosen, jnp.where(routes_ref[t : t + 1] == expert, F32(1), F32(0)))
    before = lax.broadcasted_iota(jnp.int32, (rows, rows), 0)
    after = lax.broadcasted_iota(jnp.int32, (rows, rows), 1)
    upto = jnp.where(before <= after, F32(1), F32(0)).astype(BF16)
    rank = jnp.dot(chosen.astype(BF16), upto, preferred_element_type=F32) - 1
    slot = jnp.where(chosen > 0, rank, F32(-1))
    place = lax.broadcasted_iota(jnp.int32, (capacity, rows), 0).astype(F32)
    for group, out in zip(groups, outs):
        for i, s in enumerate(group):
            hit = jnp.where(slot[s : s + 1] == place, F32(1), F32(0))
            out[i * capacity : (i + 1) * capacity] = hit.astype(BF16)


def plan(routes, groups):
    top, rows = routes.shape
    capacity = rows * 3 // 8
    return call(
        functools.partial(plan_kernel, groups=groups),
        "plan",
        tuple(array((len(group) * capacity, rows)) for group in groups),
        (routes,),
        4,
        0,
    )


def project_rows(blocks, gain_ref, w_ref, q_ref, kv_ref, normed, head_dim):
    rows = blocks[0].shape[0]
    for i, block in enumerate(blocks):
        normed[i * rows : (i + 1) * rows] = rms_norm(block[...], gain_ref[0:1])
    for h in range(q_ref.shape[1] // head_dim):
        columns = slice(3 * h * head_dim, 3 * (h + 1) * head_dim)
        out = jnp.dot(normed[...], w_ref[:, columns], preferred_element_type=F32).astype(BF16)
        q_ref[:, h * head_dim : (h + 1) * head_dim] = out[:, :head_dim]
        kv_ref[:, 2 * h * head_dim : 2 * (h + 1) * head_dim] = out[:, head_dim:]


def project_kernel(*refs, head_dim):
    *blocks, gain_ref, w_ref, q_ref, kv_ref, normed = refs
    project_rows(blocks, gain_ref, w_ref, q_ref, kv_ref, normed, head_dim)


def project(blocks, gains, w_flat, heads, head_dim):
    rows, width = len(blocks) * blocks[0].shape[0], blocks[0].shape[1]
    return call(
        functools.partial(project_kernel, head_dim=head_dim),
        "project",
        (array((rows, heads * head_dim)), array((rows, heads * 2 * head_dim))),
        (*blocks, gains, w_flat),
        12,
        0,
        [pltpu.VMEM((rows, width), BF16)],
    )


def attend_rows(first, seg_ref, queries, kvs, keep_ref, send_ref, bias, head_dim):
    block = keep_ref.shape[0]
    me = lax.axis_index("seq")
    row = jnp.concatenate(
        [
            seg_ref[:, pl.ds(pl.multiple_of((me ^ k) * block, block), block)]
            for k in range(seg_ref.shape[1] // block)
        ],
        axis=1,
    ).astype(F32)
    column = jnp.broadcast_to(row, (8, row.shape[1])).T[first : first + 2 * block, 0:1]
    bias[...] = jnp.where(column == row, F32(0), F32(-1e30))
    factor = math.log2(math.e) / math.sqrt(head_dim)
    for h in range(queries[0].shape[1] // head_dim):
        q_cols = slice(h * head_dim, (h + 1) * head_dim)
        k_cols = slice(2 * h * head_dim, (2 * h + 1) * head_dim)
        v_cols = slice((2 * h + 1) * head_dim, (2 * h + 2) * head_dim)
        query = jnp.concatenate([ref[:, q_cols] for ref in queries], axis=0)
        key = jnp.concatenate([ref[:, k_cols] for ref in kvs], axis=0)
        value = jnp.concatenate([ref[:, v_cols] for ref in kvs], axis=0)
        scores = lax.dot_general(
            query, key, (((1,), (1,)), ((), ())), preferred_element_type=F32
        )
        scores = scores + bias[...]
        top = jnp.max(scores, axis=-1, keepdims=True)
        weights = jnp.exp2((scores - top) * factor)
        total = jnp.sum(weights, axis=-1, keepdims=True)
        context = jnp.dot(weights.astype(BF16), value, preferred_element_type=F32)
        context = (context / total).astype(BF16)
        keep_ref[:, q_cols] = context[:block]
        send_ref[:, q_cols] = context[block:]


def attend_near_kernel(seg, q, kv_near, kv_far, kv_last, keep, send, bias, *, head_dim):
    attend_rows(0, seg, [q], [kv_near, kv_far, kv_last], keep, send, bias, head_dim)


def attend_near(segments, q, kvs, head_dim):
    rows, cols = q.shape
    group_len = segments.shape[1]
    return call(
        functools.partial(attend_near_kernel, head_dim=head_dim),
        "attend_near",
        (array((rows // 2, cols)),) * 2,
        (segments, q, *kvs),
        12,
        1 << 34,
        [pltpu.VMEM((rows, group_len), F32)],
    )


def attend_far_kernel(
    seg, q_far, kv_near, kv_far, block, gain, w_ref, keep, send, kv, q, normed, bias, *, head_dim
):
    project_rows([block], gain, w_ref, q, kv, normed, head_dim)
    first = kv_near.shape[0]
    attend_rows(first, seg, [q_far, q], [kv_near, kv_far, kv], keep, send, bias, head_dim)


def attend_far(segments, q_far, kv_near, kv_far, block, gains, w_flat, head_dim):
    rows, cols = q_far.shape
    group_len = segments.shape[1]
    return call(
        functools.partial(attend_far_kernel, head_dim=head_dim),
        "attend_far",
        (array((rows, cols)),) * 2 + (array((rows, 2 * cols)),),
        (segments, q_far, kv_near, kv_far, block, gains, w_flat),
        12,
        0,
        [
            pltpu.VMEM((rows, cols), BF16),
            pltpu.VMEM(block.shape, BF16),
            pltpu.VMEM((2 * rows, group_len), F32),
        ],
    )


def out_project_kernel(mine_ref, theirs_ref, w_mine, w_theirs, out_ref):
    out = jnp.dot(mine_ref[...], w_mine[...], preferred_element_type=F32)
    out = out + jnp.dot(theirs_ref[...], w_theirs[...], preferred_element_type=F32)
    out_ref[...] = out.astype(out_ref.dtype)


def out_project(mine, theirs, w_mine, w_theirs, dtype):
    rows, depth = mine.shape
    width = w_mine.shape[1]
    return call(
        out_project_kernel,
        "out_project",
        array((rows, width), dtype),
        (mine, theirs, w_mine, w_theirs),
        8,
        0,
    )


def join_rows(refs, spans, out):
    at = 0
    for ref, (low, high) in zip(refs, spans):
        out[at : at + high - low] = ref[low:high]
        at += high - low


def join_kernel(*refs, spans):
    join_rows(refs[:-1], spans, refs[-1])


def split(parts):
    arrays = tuple(part[0] for part in parts)
    spans = tuple((low, high) for _, low, high in parts)
    return arrays, spans, sum(high - low for low, high in spans)


def full(value):
    return (value, 0, value.shape[0])


def join(parts):
    arrays, spans, rows = split(parts)
    return call(
        functools.partial(join_kernel, spans=spans),
        "join",
        array((rows, arrays[0].shape[1])),
        arrays,
        4,
        0,
    )


def pages_out_kernel(owner_ref, *refs, count):
    *blocks, rows, pages = refs
    blocks, outs = blocks[: -(count // 4)], blocks[-(count // 4) :]
    size = blocks[0].shape[0]
    page_len = outs[0].shape[0]
    seq_me, blk_me = lax.axis_index("seq"), lax.axis_index("blk")
    for k, block in enumerate(blocks):
        rows[pl.ds(pl.multiple_of((seq_me ^ k) * size, size), size)] = block[...]
    for j in range(count):
        step = owner_ref[0, j] ^ blk_me

        @pl.when(step % 4 == seq_me)
        def _(j=j, step=step):
            pages[step // 4] = rows[j * page_len : (j + 1) * page_len]

    for k, out in enumerate(outs):
        out[...] = pages[k]


def pages_out(owners, blocks):
    count = owners.shape[1]
    size, width = blocks[0].shape
    group_len = len(blocks) * size
    page_len = group_len // count
    return call(
        functools.partial(pages_out_kernel, count=count),
        "pages_out",
        (array((page_len, width)),) * (count // 4),
        (owners, *blocks),
        8,
        0,
        [pltpu.VMEM((group_len, width), BF16), pltpu.VMEM((count // 4, page_len, width), BF16)],
        scalars=1,
    )


def to_owner(page, number):
    seq_count, blk_count = lax.axis_size("seq"), lax.axis_size("blk")
    pairs = [
        (i * blk_count + b, i * blk_count + (b ^ (4 * number + i)))
        for i in range(seq_count)
        for b in range(blk_count)
    ]
    return lax.ppermute(page, ("seq", "blk"), pairs)


def cache_kernel(mine_ref, theirs_ref, gain_ref, w_ref, out_ref, rows, *, head_dim):
    count, page_len = out_ref.shape[1:3]
    seq_me, blk_me = lax.axis_index("seq"), lax.axis_index("blk")
    half = count // 4 * page_len
    for core, ref in enumerate((mine_ref, theirs_ref)):
        for chip in range(2):
            for k in range(count // 4):
                start = (blk_me ^ (4 * k + (seq_me ^ (2 * chip + core)))) * page_len
                page = ref[chip * half + k * page_len : chip * half + (k + 1) * page_len]
                rows[pl.ds(pl.multiple_of(start, page_len), page_len)] = page
    rows[...] = rms_norm(rows[...], gain_ref[0:1])
    for h in range(out_ref.shape[3] // (2 * head_dim)):
        columns = slice((3 * h + 1) * head_dim, 3 * (h + 1) * head_dim)
        out = jnp.dot(rows[...], w_ref[:, columns], preferred_element_type=F32).astype(BF16)
        out = out.reshape(count, page_len, 2 * head_dim)
        out_ref[0, :, :, 2 * h * head_dim : 2 * (h + 1) * head_dim] = out


def cache(mine, theirs, gains, w_flat, count, heads, head_dim):
    rows, width = mine.shape
    return call(
        functools.partial(cache_kernel, head_dim=head_dim),
        "cache",
        array((1, count, 2 * rows // count, heads * 2 * head_dim)),
        (mine, theirs, gains, w_flat),
        16,
        0,
        [pltpu.VMEM((2 * rows, width), BF16)],
    )


def pick_rows(pick, ffn_in, outs):
    picked = jnp.dot(pick, ffn_in, preferred_element_type=F32).astype(BF16)
    at = 0
    for out in outs:
        out[...] = picked[at : at + out.shape[0]]
        at += out.shape[0]


def dispatch_kernel(own_ref, mixed_ref, far_ref, gain_ref, pick_ref, resid_ref, ffn_ref, *outs):
    resid = own_ref[...].astype(F32) + mixed_ref[...] + far_ref[...].astype(F32)
    resid = resid.astype(BF16)
    resid_ref[...] = resid
    ffn_in = rms_norm(resid, gain_ref[1:2])
    ffn_ref[...] = ffn_in
    pick_rows(pick_ref[...], ffn_in, outs)


def dispatch(own, mixed, far, gains, pick, count):
    rows, width = own.shape
    capacity = pick.shape[0] // count
    return call(
        dispatch_kernel,
        "dispatch",
        (array((rows, width)),) * 2 + (array((capacity, width)),) * count,
        (own, mixed, far, gains, pick),
        max(10, pick.shape[0] * width * 12 >> 20),
        0,
    )


def dispatch_more_kernel(ffn_ref, pick_ref, *outs):
    pick_rows(pick_ref[...], ffn_ref[...], outs)


def dispatch_more(ffn_in, pick, sizes):
    width = ffn_in.shape[1]
    return call(
        dispatch_more_kernel,
        "dispatch_more",
        tuple(array((size, width)) for size in sizes),
        (ffn_in, pick),
        max(10, pick.shape[0] * width * 12 >> 20),
        1 << 34,
    )


def weigh_kernel(ffn_ref, router_ref, *refs, groups):
    logits = lax.dot_general(
        router_ref[...], ffn_ref[...], (((1,), (1,)), ((), ())), preferred_element_type=F32
    )
    gates = jax.nn.sigmoid(logits).astype(BF16)
    experts = gates.shape[0]
    step = lax.broadcasted_iota(jnp.int32, (experts, experts), 0)
    expert = lax.broadcasted_iota(jnp.int32, (experts, experts), 1)
    order = jnp.where(lax.axis_index("blk") ^ step == expert, F32(1), F32(0)).astype(BF16)
    gates = jnp.dot(order, gates, preferred_element_type=F32)
    for group, pick, out in zip(groups, refs[: len(groups)], refs[len(groups) :]):
        capacity = pick.shape[0] // len(group)
        parts = [
            pick[i * capacity : (i + 1) * capacity].astype(F32) * gates[s : s + 1]
            for i, s in enumerate(group)
        ]
        out[...] = jnp.concatenate(parts, axis=0).T.astype(BF16)


def weigh(ffn_in, router, picks, groups):
    return call(
        functools.partial(weigh_kernel, groups=groups),
        "weigh",
        tuple(array(pick.shape[::-1]) for pick in picks),
        (ffn_in, router, *picks),
        8,
        0,
    )


def expert_kernel(*refs, spans):
    count = len(spans)
    in_ref, down_ref = refs[count : count + 2]
    *outs, rows, hidden = refs[count + 2 :]
    ff, width = down_ref.shape
    join_rows(refs[:count], spans, rows)
    tile = min(ff, 512)
    for start in range(0, ff, tile):
        gate = jnp.dot(rows[...], in_ref[:, start : start + tile], preferred_element_type=F32)
        up = jnp.dot(
            rows[...], in_ref[:, ff + start : ff + start + tile], preferred_element_type=F32
        )
        hidden[:, start : start + tile] = (jax.nn.silu(gate) * up).astype(BF16)
    for start in range(0, width, tile):
        part = jnp.dot(hidden[...], down_ref[:, start : start + tile], preferred_element_type=F32)
        at = 0
        for out in outs:
            out[:, start : start + tile] = part[at : at + out.shape[0]].astype(BF16)
            at += out.shape[0]


def expert(parts, gate_up, down):
    arrays, spans, rows = split(parts)
    ff, width = down.shape
    return call(
        functools.partial(expert_kernel, spans=spans),
        "expert",
        tuple(array((high - low, width)) for low, high in spans),
        (*arrays, gate_up, down),
        max(8, rows * 20480 >> 20),
        1 << 35,
        [pltpu.VMEM((rows, width), BF16), pltpu.VMEM((rows, ff), BF16)],
    )


def combine_kernel(base_ref, weigh_ref, *refs, spans):
    *ins, out_ref, rows = refs
    join_rows(ins, spans, rows)
    total = jnp.dot(weigh_ref[...], rows[...], preferred_element_type=F32)
    out_ref[...] = (base_ref[...].astype(F32) + total).astype(out_ref.dtype)


def combine(base, weights, parts, dtype):
    arrays, spans, rows = split(parts)
    return call(
        functools.partial(combine_kernel, spans=spans),
        "combine",
        array(base.shape, dtype),
        (base, weights, *arrays),
        max(8, rows * 16384 >> 20),
        0,
        [pltpu.VMEM((rows, base.shape[1]), BF16)],
    )


def on_device(
    residual_in,
    segment_ids,
    attn_gain,
    w_qkv,
    w_out,
    ffn_gain,
    w_router,
    routes,
    w_gate_up,
    w_down,
    page_owner,
):
    own = residual_in[0]
    width = own.shape[1]
    heads_here = w_qkv.shape[1]
    head_dim = w_out.shape[1]
    blk_count = lax.axis_size("blk")

    slots = own.shape[0] * 3 // 8
    half = (4 + blk_count) // 2
    near, first, last = tuple(range(4)), tuple(range(4, half)), tuple(range(half, blk_count))
    groups = (first, (*near, *last))
    picks = plan(routes[0].T, groups)

    far = swap(own, "seq", 2)
    w_mine = w_out.reshape(heads_here * head_dim, width)
    core = swap(own, "seq", 1)
    w_theirs = swap(w_mine, "seq", 1)
    gains = jnp.stack([attn_gain, ffn_gain])

    w_flat = held(w_qkv.reshape(width, heads_here * 3 * head_dim))
    q_near, kv_near = project((own, core), gains, w_flat, heads_here, head_dim)
    far, q_near, kv_near = lax.optimization_barrier((far, q_near, kv_near))
    far_core = swap(far, "seq", 1)
    q_far, kv_far = project((far,), gains, w_flat, heads_here, head_dim)
    keep_far, send_far, kv_last = attend_far(
        segment_ids, q_far, kv_near, kv_far, far_core, gains, w_flat, head_dim
    )
    w_mine, w_theirs = held(w_mine), held(w_theirs)
    theirs_far = swap(send_far, "seq", 1)
    outgoing = pages_out(page_owner, (own, core, far, far_core))
    theirs_far, outgoing = lax.optimization_barrier((theirs_far, outgoing))
    far_sum = out_project(keep_far, theirs_far, w_mine, w_theirs, BF16)
    from_far = swap(far_sum, "seq", 2)
    keep, send = attend_near(segment_ids, q_near, (kv_near, kv_far, kv_last), head_dim)
    send, outgoing = lax.optimization_barrier((send, outgoing))
    arrived = [to_owner(page, k) for k, page in enumerate(outgoing)]
    mixed = out_project(keep, swap(send, "seq", 1), w_mine, w_theirs, F32)

    gate_up, down = held(w_gate_up[0]), held(w_down[0])

    def there(group, blocks):
        pairs = zip(group, blocks)
        return tuple(swap(block, "blk", step) if step else block for step, block in pairs)

    def work(blocks):
        return expert([full(block) for block in blocks], gate_up, down)

    resid, ffn_in, *sent_first = dispatch(own, mixed, from_far, gains, picks[0], len(first))
    rows_first = there(first, sent_first)
    sent = dispatch_more(ffn_in, picks[1], (slots,) * len(groups[1]))
    sent_near, sent_last = sent[: len(near)], sent[len(near) :]
    sent_near, arrived = lax.optimization_barrier((sent_near, arrived))
    rows_near = there(near, sent_near)
    share = join([full(page) for page in arrived])
    share_far = swap(share, "seq", 2)
    rows_last = there(last, sent_last)
    first_out = work(rows_first)
    back_first = there(first, first_out)
    rows_near, first_out, share_far = lax.optimization_barrier((rows_near, first_out, share_far))
    both = join([full(share), full(share_far)])
    both_core = swap(both, "seq", 1)
    near_out = work(rows_near)
    rows_last, both_core = lax.optimization_barrier((rows_last, both_core))
    last_out = work(rows_last)
    back_last = there(last, last_out)
    near_out, last_out, both_core = lax.optimization_barrier((near_out, last_out, both_core))
    back_near = there(near, near_out)
    kv_cache = cache(both, both_core, gains, w_flat, blk_count, heads_here, head_dim)

    weights = weigh(ffn_in, w_router.T, picks, groups)
    total = combine(resid, weights[0], [full(block) for block in back_first], F32)
    kv_cache, total = lax.optimization_barrier((kv_cache, total))
    parts = [full(block) for block in (*back_near, *back_last)]
    total = combine(total, weights[1], parts, BF16)
    return (total[None], kv_cache)


def solution(mesh):
    in_specs = (
        P("blk", "seq", None),
        P("blk", None),
        P(),
        P(None, "seq", None),
        P("seq", None, None),
        P(),
        P(),
        P("blk", "seq", None),
        P("blk", None, None),
        P("blk", None, None),
        P("blk", None),
    )
    out_specs = (P("blk", "seq", None), P("blk", None, None, "seq"))
    return jax.shard_map(
        on_device, mesh=mesh, in_specs=in_specs, out_specs=out_specs, check_vma=False
    )
```

```python
import functools
import math

import jax
import jax.numpy as jnp
from jax import lax
from jax.experimental import pallas as pl
from jax.experimental.pallas import tpu as pltpu
from jax.sharding import PartitionSpec as P

EPS = 1e-06
F32 = jnp.float32
BF16 = jnp.bfloat16
VMEM_SPEC = pl.BlockSpec(memory_space=pltpu.VMEM)
SMEM_SPEC = pl.BlockSpec(memory_space=pltpu.SMEM)


def rms_norm(value, gain):
    wide = value.astype(F32)
    scale = lax.rsqrt(jnp.mean(wide * wide, axis=-1, keepdims=True) + EPS)
    return (wide * scale * gain.astype(F32)).astype(BF16)


def swap(value, axis, step):
    size = lax.axis_size(axis)
    return lax.ppermute(value, axis, [(i, i ^ step) for i in range(size)])


def held(value):
    return pltpu.with_memory_space_constraint(value, pltpu.VMEM)


def array(shape, dtype=BF16):
    return jax.ShapeDtypeStruct(shape, dtype)


def call(kernel, name, out_shape, args, mib, flops, scratch=(), scalars=0):
    return pl.pallas_call(
        kernel,
        out_shape=out_shape,
        in_specs=[SMEM_SPEC] * scalars + [VMEM_SPEC] * (len(args) - scalars),
        scratch_shapes=scratch,
        compiler_params=pltpu.CompilerParams(vmem_limit_bytes=mib << 20),
        cost_estimate=pl.CostEstimate(flops=flops, bytes_accessed=0, transcendentals=0),
        name=name,
    )(*args)


def plan_kernel(routes_ref, *outs, groups):
    top, rows = routes_ref.shape
    count = sum(map(len, groups))
    capacity = outs[0].shape[0] // len(groups[0])
    expert = lax.axis_index("blk") ^ lax.broadcasted_iota(jnp.int32, (count, rows), 0)
    chosen = jnp.zeros((count, rows), F32)
    for t in range(top):
        chosen = jnp.maximum(chosen, jnp.where(routes_ref[t : t + 1] == expert, F32(1), F32(0)))
    before = lax.broadcasted_iota(jnp.int32, (rows, rows), 0)
    after = lax.broadcasted_iota(jnp.int32, (rows, rows), 1)
    upto = jnp.where(before <= after, F32(1), F32(0)).astype(BF16)
    rank = jnp.dot(chosen.astype(BF16), upto, preferred_element_type=F32) - 1
    slot = jnp.where(chosen > 0, rank, F32(-1))
    place = lax.broadcasted_iota(jnp.int32, (capacity, rows), 0).astype(F32)
    for group, out in zip(groups, outs):
        for i, s in enumerate(group):
            hit = jnp.where(slot[s : s + 1] == place, F32(1), F32(0))
            out[i * capacity : (i + 1) * capacity] = hit.astype(BF16)


def plan(routes, groups):
    top, rows = routes.shape
    capacity = rows * 3 // 8
    return call(
        functools.partial(plan_kernel, groups=groups),
        "plan",
        tuple(array((len(group) * capacity, rows)) for group in groups),
        (routes,),
        4,
        0,
    )


def project_rows(blocks, gain_ref, w_ref, q_ref, kv_ref, normed, head_dim):
    rows = blocks[0].shape[0]
    for i, block in enumerate(blocks):
        normed[i * rows : (i + 1) * rows] = rms_norm(block[...], gain_ref[0:1])
    for h in range(q_ref.shape[1] // head_dim):
        columns = slice(3 * h * head_dim, 3 * (h + 1) * head_dim)
        out = jnp.dot(normed[...], w_ref[:, columns], preferred_element_type=F32).astype(BF16)
        q_ref[:, h * head_dim : (h + 1) * head_dim] = out[:, :head_dim]
        kv_ref[:, 2 * h * head_dim : 2 * (h + 1) * head_dim] = out[:, head_dim:]


def project_kernel(*refs, head_dim):
    *blocks, gain_ref, w_ref, q_ref, kv_ref, normed = refs
    project_rows(blocks, gain_ref, w_ref, q_ref, kv_ref, normed, head_dim)


def project(blocks, gains, w_flat, heads, head_dim):
    rows, width = len(blocks) * blocks[0].shape[0], blocks[0].shape[1]
    return call(
        functools.partial(project_kernel, head_dim=head_dim),
        "project",
        (array((rows, heads * head_dim)), array((rows, heads * 2 * head_dim))),
        (*blocks, gains, w_flat),
        12,
        0,
        [pltpu.VMEM((rows, width), BF16)],
    )


def attend_rows(first, seg_ref, queries, kvs, keep_ref, send_ref, bias, head_dim):
    block = keep_ref.shape[0]
    me = lax.axis_index("seq")
    row = jnp.concatenate(
        [
            seg_ref[:, pl.ds(pl.multiple_of((me ^ k) * block, block), block)]
            for k in range(seg_ref.shape[1] // block)
        ],
        axis=1,
    ).astype(F32)
    column = jnp.broadcast_to(row, (8, row.shape[1])).T[first : first + 2 * block, 0:1]
    bias[...] = jnp.where(column == row, F32(0), F32(-1e30))
    factor = math.log2(math.e) / math.sqrt(head_dim)
    for h in range(queries[0].shape[1] // head_dim):
        q_cols = slice(h * head_dim, (h + 1) * head_dim)
        k_cols = slice(2 * h * head_dim, (2 * h + 1) * head_dim)
        v_cols = slice((2 * h + 1) * head_dim, (2 * h + 2) * head_dim)
        query = jnp.concatenate([ref[:, q_cols] for ref in queries], axis=0)
        key = jnp.concatenate([ref[:, k_cols] for ref in kvs], axis=0)
        value = jnp.concatenate([ref[:, v_cols] for ref in kvs], axis=0)
        scores = lax.dot_general(
            query, key, (((1,), (1,)), ((), ())), preferred_element_type=F32
        )
        scores = scores + bias[...]
        top = jnp.max(scores, axis=-1, keepdims=True)
        weights = jnp.exp2((scores - top) * factor)
        total = jnp.sum(weights, axis=-1, keepdims=True)
        context = jnp.dot(weights.astype(BF16), value, preferred_element_type=F32)
        context = (context / total).astype(BF16)
        keep_ref[:, q_cols] = context[:block]
        send_ref[:, q_cols] = context[block:]


def attend_near_kernel(seg, q, kv_near, kv_far, kv_last, keep, send, bias, *, head_dim):
    attend_rows(0, seg, [q], [kv_near, kv_far, kv_last], keep, send, bias, head_dim)


def attend_near(segments, q, kvs, head_dim):
    rows, cols = q.shape
    group_len = segments.shape[1]
    return call(
        functools.partial(attend_near_kernel, head_dim=head_dim),
        "attend_near",
        (array((rows // 2, cols)),) * 2,
        (segments, q, *kvs),
        12,
        1 << 34,
        [pltpu.VMEM((rows, group_len), F32)],
    )


def attend_far_kernel(
    seg, q_far, kv_near, kv_far, block, gain, w_ref, keep, send, kv, q, normed, bias, *, head_dim
):
    project_rows([block], gain, w_ref, q, kv, normed, head_dim)
    first = kv_near.shape[0]
    attend_rows(first, seg, [q_far, q], [kv_near, kv_far, kv], keep, send, bias, head_dim)


def attend_far(segments, q_far, kv_near, kv_far, block, gains, w_flat, head_dim):
    rows, cols = q_far.shape
    group_len = segments.shape[1]
    return call(
        functools.partial(attend_far_kernel, head_dim=head_dim),
        "attend_far",
        (array((rows, cols)),) * 2 + (array((rows, 2 * cols)),),
        (segments, q_far, kv_near, kv_far, block, gains, w_flat),
        12,
        0,
        [
            pltpu.VMEM((rows, cols), BF16),
            pltpu.VMEM(block.shape, BF16),
            pltpu.VMEM((2 * rows, group_len), F32),
        ],
    )


def out_project_kernel(mine_ref, theirs_ref, w_mine, w_theirs, out_ref):
    out = jnp.dot(mine_ref[...], w_mine[...], preferred_element_type=F32)
    out = out + jnp.dot(theirs_ref[...], w_theirs[...], preferred_element_type=F32)
    out_ref[...] = out.astype(out_ref.dtype)


def out_project(mine, theirs, w_mine, w_theirs, dtype):
    rows, depth = mine.shape
    width = w_mine.shape[1]
    return call(
        out_project_kernel,
        "out_project",
        array((rows, width), dtype),
        (mine, theirs, w_mine, w_theirs),
        8,
        0,
    )


def join_rows(refs, spans, out):
    at = 0
    for ref, (low, high) in zip(refs, spans):
        out[at : at + high - low] = ref[low:high]
        at += high - low


def join_kernel(*refs, spans):
    join_rows(refs[:-1], spans, refs[-1])


def split(parts):
    arrays = tuple(part[0] for part in parts)
    spans = tuple((low, high) for _, low, high in parts)
    return arrays, spans, sum(high - low for low, high in spans)


def full(value):
    return (value, 0, value.shape[0])


def join(parts):
    arrays, spans, rows = split(parts)
    return call(
        functools.partial(join_kernel, spans=spans),
        "join",
        array((rows, arrays[0].shape[1])),
        arrays,
        4,
        0,
    )


def pages_out_kernel(owner_ref, *refs, count):
    *blocks, rows, pages = refs
    blocks, outs = blocks[: -(count // 4)], blocks[-(count // 4) :]
    size = blocks[0].shape[0]
    page_len = outs[0].shape[0]
    seq_me, blk_me = lax.axis_index("seq"), lax.axis_index("blk")
    for k, block in enumerate(blocks):
        rows[pl.ds(pl.multiple_of((seq_me ^ k) * size, size), size)] = block[...]
    for j in range(count):
        step = owner_ref[0, j] ^ blk_me

        @pl.when(step % 4 == seq_me)
        def _(j=j, step=step):
            pages[count // 4 - 1 - step // 4] = rows[j * page_len : (j + 1) * page_len]

    for k, out in enumerate(outs):
        out[...] = pages[k]


def pages_out(owners, blocks):
    count = owners.shape[1]
    size, width = blocks[0].shape
    group_len = len(blocks) * size
    page_len = group_len // count
    return call(
        functools.partial(pages_out_kernel, count=count),
        "pages_out",
        (array((page_len, width)),) * (count // 4),
        (owners, *blocks),
        8,
        0,
        [pltpu.VMEM((group_len, width), BF16), pltpu.VMEM((count // 4, page_len, width), BF16)],
        scalars=1,
    )


def to_owner(page, number):
    seq_count, blk_count = lax.axis_size("seq"), lax.axis_size("blk")
    k = blk_count // 4 - 1 - number
    pairs = [
        (i * blk_count + b, i * blk_count + (b ^ (4 * k + i)))
        for i in range(seq_count)
        for b in range(blk_count)
    ]
    return lax.ppermute(page, ("seq", "blk"), pairs)


def cache_kernel(mine_ref, theirs_ref, gain_ref, w_ref, out_ref, rows, *, head_dim):
    count, page_len = out_ref.shape[1:3]
    seq_me, blk_me = lax.axis_index("seq"), lax.axis_index("blk")
    half = count // 4 * page_len
    for core, ref in enumerate((mine_ref, theirs_ref)):
        for chip in range(2):
            for k in range(count // 4):
                step = 4 * (count // 4 - 1 - k) + (seq_me ^ (2 * chip + core))
                start = (blk_me ^ step) * page_len
                page = ref[chip * half + k * page_len : chip * half + (k + 1) * page_len]
                rows[pl.ds(pl.multiple_of(start, page_len), page_len)] = page
    rows[...] = rms_norm(rows[...], gain_ref[0:1])
    for h in range(out_ref.shape[3] // (2 * head_dim)):
        columns = slice((3 * h + 1) * head_dim, 3 * (h + 1) * head_dim)
        out = jnp.dot(rows[...], w_ref[:, columns], preferred_element_type=F32).astype(BF16)
        out = out.reshape(count, page_len, 2 * head_dim)
        out_ref[0, :, :, 2 * h * head_dim : 2 * (h + 1) * head_dim] = out


def cache(mine, theirs, gains, w_flat, count, heads, head_dim):
    rows, width = mine.shape
    return call(
        functools.partial(cache_kernel, head_dim=head_dim),
        "cache",
        array((1, count, 2 * rows // count, heads * 2 * head_dim)),
        (mine, theirs, gains, w_flat),
        16,
        0,
        [pltpu.VMEM((2 * rows, width), BF16)],
    )


def pick_rows(pick, ffn_in, outs):
    picked = jnp.dot(pick, ffn_in, preferred_element_type=F32).astype(BF16)
    at = 0
    for out in outs:
        out[...] = picked[at : at + out.shape[0]]
        at += out.shape[0]


def dispatch_kernel(own_ref, mixed_ref, far_ref, gain_ref, pick_ref, resid_ref, ffn_ref, *outs):
    resid = own_ref[...].astype(F32) + mixed_ref[...] + far_ref[...].astype(F32)
    resid = resid.astype(BF16)
    resid_ref[...] = resid
    ffn_in = rms_norm(resid, gain_ref[1:2])
    ffn_ref[...] = ffn_in
    pick_rows(pick_ref[...], ffn_in, outs)


def dispatch(own, mixed, far, gains, pick, count):
    rows, width = own.shape
    capacity = pick.shape[0] // count
    return call(
        dispatch_kernel,
        "dispatch",
        (array((rows, width)),) * 2 + (array((capacity, width)),) * count,
        (own, mixed, far, gains, pick),
        max(10, pick.shape[0] * width * 12 >> 20),
        0,
    )


def dispatch_more_kernel(ffn_ref, pick_ref, *outs):
    pick_rows(pick_ref[...], ffn_ref[...], outs)


def dispatch_more(ffn_in, pick, sizes):
    width = ffn_in.shape[1]
    return call(
        dispatch_more_kernel,
        "dispatch_more",
        tuple(array((size, width)) for size in sizes),
        (ffn_in, pick),
        max(10, pick.shape[0] * width * 12 >> 20),
        1 << 34,
    )


def weigh_kernel(ffn_ref, router_ref, *refs, groups, sums):
    logits = lax.dot_general(
        router_ref[...], ffn_ref[...], (((1,), (1,)), ((), ())), preferred_element_type=F32
    )
    gates = jax.nn.sigmoid(logits).astype(BF16)
    experts = gates.shape[0]
    step = lax.broadcasted_iota(jnp.int32, (experts, experts), 0)
    expert = lax.broadcasted_iota(jnp.int32, (experts, experts), 1)
    order = jnp.where(lax.axis_index("blk") ^ step == expert, F32(1), F32(0)).astype(BF16)
    gates = jnp.dot(order, gates, preferred_element_type=F32)
    picks, outs = refs[: len(groups)], refs[len(groups) :]
    capacity = picks[0].shape[0] // len(groups[0])
    pick_of = {
        step: pick[i * capacity : (i + 1) * capacity]
        for group, pick in zip(groups, picks)
        for i, step in enumerate(group)
    }
    for steps, out in zip(sums, outs):
        parts = [pick_of[s].astype(F32) * gates[s : s + 1] for s in steps]
        out[...] = jnp.concatenate(parts, axis=0).T.astype(BF16)


def weigh(ffn_in, router, picks, groups, sums):
    capacity, rows = picks[0].shape[0] // len(groups[0]), ffn_in.shape[0]
    return call(
        functools.partial(weigh_kernel, groups=groups, sums=sums),
        "weigh",
        tuple(array((rows, len(steps) * capacity)) for steps in sums),
        (ffn_in, router, *picks),
        8,
        0,
    )


def expert_kernel(*refs, spans):
    count = len(spans)
    in_ref, down_ref = refs[count : count + 2]
    *outs, rows, hidden = refs[count + 2 :]
    ff, width = down_ref.shape
    join_rows(refs[:count], spans, rows)
    tile = min(ff, 512)
    for start in range(0, ff, tile):
        gate = jnp.dot(rows[...], in_ref[:, start : start + tile], preferred_element_type=F32)
        up = jnp.dot(
            rows[...], in_ref[:, ff + start : ff + start + tile], preferred_element_type=F32
        )
        hidden[:, start : start + tile] = (jax.nn.silu(gate) * up).astype(BF16)
    for start in range(0, width, tile):
        part = jnp.dot(hidden[...], down_ref[:, start : start + tile], preferred_element_type=F32)
        at = 0
        for out in outs:
            out[:, start : start + tile] = part[at : at + out.shape[0]].astype(BF16)
            at += out.shape[0]


def expert(parts, gate_up, down):
    arrays, spans, rows = split(parts)
    ff, width = down.shape
    return call(
        functools.partial(expert_kernel, spans=spans),
        "expert",
        tuple(array((high - low, width)) for low, high in spans),
        (*arrays, gate_up, down),
        max(8, rows * 20480 >> 20),
        1 << 35,
        [pltpu.VMEM((rows, width), BF16), pltpu.VMEM((rows, ff), BF16)],
    )


def combine_kernel(base_ref, weigh_ref, *refs, spans):
    *ins, out_ref, rows = refs
    join_rows(ins, spans, rows)
    total = jnp.dot(weigh_ref[...], rows[...], preferred_element_type=F32)
    out_ref[...] = (base_ref[...].astype(F32) + total).astype(out_ref.dtype)


def combine(base, weights, parts, dtype):
    arrays, spans, rows = split(parts)
    return call(
        functools.partial(combine_kernel, spans=spans),
        "combine",
        array(base.shape, dtype),
        (base, weights, *arrays),
        max(8, rows * 16384 >> 20),
        0,
        [pltpu.VMEM((rows, base.shape[1]), BF16)],
    )


def on_device(
    residual_in,
    segment_ids,
    attn_gain,
    w_qkv,
    w_out,
    ffn_gain,
    w_router,
    routes,
    w_gate_up,
    w_down,
    page_owner,
):
    own = residual_in[0]
    width = own.shape[1]
    heads_here = w_qkv.shape[1]
    head_dim = w_out.shape[1]
    blk_count = lax.axis_size("blk")

    slots = own.shape[0] * 3 // 8
    half = (4 + blk_count) // 2
    near, first, last = tuple(range(4)), tuple(range(4, half)), tuple(range(half, blk_count))
    groups = (first, (*near, *last))
    picks = plan(routes[0].T, groups)

    far = swap(own, "seq", 2)
    w_mine = w_out.reshape(heads_here * head_dim, width)
    core = swap(own, "seq", 1)
    w_theirs = swap(w_mine, "seq", 1)
    gains = jnp.stack([attn_gain, ffn_gain])

    w_flat = held(w_qkv.reshape(width, heads_here * 3 * head_dim))
    q_near, kv_near = project((own, core), gains, w_flat, heads_here, head_dim)
    far, q_near, kv_near = lax.optimization_barrier((far, q_near, kv_near))
    far_core = swap(far, "seq", 1)
    q_far, kv_far = project((far,), gains, w_flat, heads_here, head_dim)
    keep_far, send_far, kv_last = attend_far(
        segment_ids, q_far, kv_near, kv_far, far_core, gains, w_flat, head_dim
    )
    w_mine, w_theirs = held(w_mine), held(w_theirs)
    theirs_far = swap(send_far, "seq", 1)
    outgoing = pages_out(page_owner, (own, core, far, far_core))
    theirs_far, outgoing = lax.optimization_barrier((theirs_far, outgoing))
    far_sum = out_project(keep_far, theirs_far, w_mine, w_theirs, BF16)
    from_far = swap(far_sum, "seq", 2)
    keep, send = attend_near(segment_ids, q_near, (kv_near, kv_far, kv_last), head_dim)
    send, outgoing = lax.optimization_barrier((send, outgoing))
    arrived = [to_owner(page, k) for k, page in enumerate(outgoing)]
    mixed = out_project(keep, swap(send, "seq", 1), w_mine, w_theirs, F32)

    gate_up, down = held(w_gate_up[0]), held(w_down[0])

    def there(group, blocks):
        pairs = zip(group, blocks)
        return tuple(swap(block, "blk", step) if step else block for step, block in pairs)

    def work(blocks):
        return expert([full(block) for block in blocks], gate_up, down)

    resid, ffn_in, *sent_first = dispatch(own, mixed, from_far, gains, picks[0], len(first))
    rows_first = there(first, sent_first)
    sent = dispatch_more(ffn_in, picks[1], (slots,) * len(groups[1]))
    sent_near, sent_last = sent[: len(near)], sent[len(near) :]
    sent_near, arrived = lax.optimization_barrier((sent_near, arrived))
    rows_near = there(near, sent_near)
    share = join([full(page) for page in arrived])
    share_far = swap(share, "seq", 2)
    rows_last = there(last, sent_last)
    first_out = work(rows_first)
    back_first = there(first, first_out)
    rows_near, first_out, share_far = lax.optimization_barrier((rows_near, first_out, share_far))
    both = join([full(share), full(share_far)])
    both_core = swap(both, "seq", 1)
    near_out = work(rows_near)
    rows_last, both_core = lax.optimization_barrier((rows_last, both_core))
    last_out = work(rows_last)
    back_last = there(last, last_out)
    near_out, last_out, both_core = lax.optimization_barrier((near_out, last_out, both_core))
    back_near = there(near, near_out)
    kv_cache = cache(both, both_core, gains, w_flat, blk_count, heads_here, head_dim)

    weights = weigh(ffn_in, w_router.T, picks, groups, (first, (*last, *near)))
    total = combine(resid, weights[0], [full(block) for block in back_first], F32)
    kv_cache, total = lax.optimization_barrier((kv_cache, total))
    parts = [full(block) for block in (*back_last, *back_near)]
    total = combine(total, weights[1], parts, BF16)
    return (total[None], kv_cache)


def solution(mesh):
    in_specs = (
        P("blk", "seq", None),
        P("blk", None),
        P(),
        P(None, "seq", None),
        P("seq", None, None),
        P(),
        P(),
        P("blk", "seq", None),
        P("blk", None, None),
        P("blk", None, None),
        P("blk", None),
    )
    out_specs = (P("blk", "seq", None), P("blk", None, None, "seq"))
    return jax.shard_map(
        on_device, mesh=mesh, in_specs=in_specs, out_specs=out_specs, check_vma=False
    )
```

```python
import functools
import math

import jax
import jax.numpy as jnp
from jax import lax
from jax.experimental import pallas as pl
from jax.experimental.pallas import tpu as pltpu
from jax.sharding import PartitionSpec as P

EPS = 1e-06
F32 = jnp.float32
BF16 = jnp.bfloat16
VMEM_SPEC = pl.BlockSpec(memory_space=pltpu.VMEM)
SMEM_SPEC = pl.BlockSpec(memory_space=pltpu.SMEM)


def rms_norm(value, gain):
    wide = value.astype(F32)
    scale = lax.rsqrt(jnp.mean(wide * wide, axis=-1, keepdims=True) + EPS)
    return (wide * scale * gain.astype(F32)).astype(BF16)


def swap(value, axis, step):
    size = lax.axis_size(axis)
    return lax.ppermute(value, axis, [(i, i ^ step) for i in range(size)])


def held(value):
    return pltpu.with_memory_space_constraint(value, pltpu.VMEM)


def array(shape, dtype=BF16):
    return jax.ShapeDtypeStruct(shape, dtype)


def call(kernel, name, out_shape, args, mib, flops, scratch=(), scalars=0):
    return pl.pallas_call(
        kernel,
        out_shape=out_shape,
        in_specs=[SMEM_SPEC] * scalars + [VMEM_SPEC] * (len(args) - scalars),
        scratch_shapes=scratch,
        compiler_params=pltpu.CompilerParams(vmem_limit_bytes=mib << 20),
        cost_estimate=pl.CostEstimate(flops=flops, bytes_accessed=0, transcendentals=0),
        name=name,
    )(*args)


def plan_kernel(routes_ref, *outs, groups):
    top, rows = routes_ref.shape
    count = sum(map(len, groups))
    capacity = outs[0].shape[0] // len(groups[0])
    expert = lax.axis_index("blk") ^ lax.broadcasted_iota(jnp.int32, (count, rows), 0)
    chosen = jnp.zeros((count, rows), F32)
    for t in range(top):
        chosen = jnp.maximum(chosen, jnp.where(routes_ref[t : t + 1] == expert, F32(1), F32(0)))
    before = lax.broadcasted_iota(jnp.int32, (rows, rows), 0)
    after = lax.broadcasted_iota(jnp.int32, (rows, rows), 1)
    upto = jnp.where(before <= after, F32(1), F32(0)).astype(BF16)
    rank = jnp.dot(chosen.astype(BF16), upto, preferred_element_type=F32) - 1
    slot = jnp.where(chosen > 0, rank, F32(-1))
    place = lax.broadcasted_iota(jnp.int32, (capacity, rows), 0).astype(F32)
    for group, out in zip(groups, outs):
        for i, s in enumerate(group):
            hit = jnp.where(slot[s : s + 1] == place, F32(1), F32(0))
            out[i * capacity : (i + 1) * capacity] = hit.astype(BF16)


def plan(routes, groups):
    top, rows = routes.shape
    capacity = rows * 3 // 8
    return call(
        functools.partial(plan_kernel, groups=groups),
        "plan",
        tuple(array((len(group) * capacity, rows)) for group in groups),
        (routes,),
        4,
        0,
    )


def project_rows(blocks, gain_ref, w_ref, q_ref, kv_ref, normed, head_dim):
    rows = blocks[0].shape[0]
    for i, block in enumerate(blocks):
        normed[i * rows : (i + 1) * rows] = rms_norm(block[...], gain_ref[0:1])
    out = jnp.dot(normed[...], w_ref[...], preferred_element_type=F32).astype(BF16)
    for h in range(q_ref.shape[1] // head_dim):
        at = 3 * h * head_dim
        q_ref[:, h * head_dim : (h + 1) * head_dim] = out[:, at : at + head_dim]
        kv_ref[:, 2 * h * head_dim : 2 * (h + 1) * head_dim] = out[
            :, at + head_dim : at + 3 * head_dim
        ]


def project_kernel(*refs, head_dim):
    *blocks, gain_ref, w_ref, q_ref, kv_ref, normed = refs
    project_rows(blocks, gain_ref, w_ref, q_ref, kv_ref, normed, head_dim)


def project(blocks, gains, w_flat, heads, head_dim):
    rows, width = len(blocks) * blocks[0].shape[0], blocks[0].shape[1]
    return call(
        functools.partial(project_kernel, head_dim=head_dim),
        "project",
        (array((rows, heads * head_dim)), array((rows, heads * 2 * head_dim))),
        (*blocks, gains, w_flat),
        12,
        0,
        [pltpu.VMEM((rows, width), BF16)],
    )


def attend_rows(first, seg_ref, queries, kvs, keep_ref, send_ref, bias, head_dim):
    block = keep_ref.shape[0]
    me = lax.axis_index("seq")
    row = jnp.concatenate(
        [
            seg_ref[:, pl.ds(pl.multiple_of((me ^ k) * block, block), block)]
            for k in range(seg_ref.shape[1] // block)
        ],
        axis=1,
    ).astype(F32)
    column = jnp.broadcast_to(row, (8, row.shape[1])).T[first : first + 2 * block, 0:1]
    bias[...] = jnp.where(column == row, F32(0), F32(-1e30))
    factor = math.log2(math.e) / math.sqrt(head_dim)
    heads = range(queries[0].shape[1] // head_dim)
    columns = [slice(h * head_dim, (h + 1) * head_dim) for h in range(2 * len(heads))]

    def rows_of(refs, cols):
        return jnp.concatenate([ref[:, cols] for ref in refs], axis=0)

    scores = [
        lax.dot_general(
            rows_of(queries, columns[h]),
            rows_of(kvs, columns[2 * h]),
            (((1,), (1,)), ((), ())),
            preferred_element_type=F32,
        )
        for h in heads
    ]
    scores = [score + bias[...] for score in scores]
    tops = [jnp.max(score, axis=-1, keepdims=True) for score in scores]
    weights = [jnp.exp2((score - top) * factor) for score, top in zip(scores, tops)]
    totals = [jnp.sum(weight, axis=-1, keepdims=True) for weight in weights]
    for h in heads:
        value = rows_of(kvs, columns[2 * h + 1])
        context = jnp.dot(weights[h].astype(BF16), value, preferred_element_type=F32)
        context = (context / totals[h]).astype(BF16)
        keep_ref[:, columns[h]] = context[:block]
        send_ref[:, columns[h]] = context[block:]


def attend_near_kernel(seg, q, kv_near, kv_far, kv_last, keep, send, bias, *, head_dim):
    attend_rows(0, seg, [q], [kv_near, kv_far, kv_last], keep, send, bias, head_dim)


def attend_near(segments, q, kvs, head_dim):
    rows, cols = q.shape
    group_len = segments.shape[1]
    return call(
        functools.partial(attend_near_kernel, head_dim=head_dim),
        "attend_near",
        (array((rows // 2, cols)),) * 2,
        (segments, q, *kvs),
        12,
        1 << 34,
        [pltpu.VMEM((rows, group_len), F32)],
    )


def attend_far_kernel(
    seg, q_far, kv_near, kv_far, block, gain, w_ref, keep, send, kv, q, normed, bias, *, head_dim
):
    project_rows([block], gain, w_ref, q, kv, normed, head_dim)
    first = kv_near.shape[0]
    attend_rows(first, seg, [q_far, q], [kv_near, kv_far, kv], keep, send, bias, head_dim)


def attend_far(segments, q_far, kv_near, kv_far, block, gains, w_flat, head_dim):
    rows, cols = q_far.shape
    group_len = segments.shape[1]
    return call(
        functools.partial(attend_far_kernel, head_dim=head_dim),
        "attend_far",
        (array((rows, cols)),) * 2 + (array((rows, 2 * cols)),),
        (segments, q_far, kv_near, kv_far, block, gains, w_flat),
        12,
        0,
        [
            pltpu.VMEM((rows, cols), BF16),
            pltpu.VMEM(block.shape, BF16),
            pltpu.VMEM((2 * rows, group_len), F32),
        ],
    )


def out_project_kernel(mine_ref, theirs_ref, w_mine, w_theirs, out_ref):
    out = jnp.dot(mine_ref[...], w_mine[...], preferred_element_type=F32)
    out = out + jnp.dot(theirs_ref[...], w_theirs[...], preferred_element_type=F32)
    out_ref[...] = out.astype(out_ref.dtype)


def out_project(mine, theirs, w_mine, w_theirs, dtype):
    rows, depth = mine.shape
    width = w_mine.shape[1]
    return call(
        out_project_kernel,
        "out_project",
        array((rows, width), dtype),
        (mine, theirs, w_mine, w_theirs),
        8,
        0,
    )


def join_rows(refs, spans, out):
    at = 0
    for ref, (low, high) in zip(refs, spans):
        out[at : at + high - low] = ref[low:high]
        at += high - low


def join_kernel(*refs, spans):
    join_rows(refs[:-1], spans, refs[-1])


def split(parts):
    arrays = tuple(part[0] for part in parts)
    spans = tuple((low, high) for _, low, high in parts)
    return arrays, spans, sum(high - low for low, high in spans)


def full(value):
    return (value, 0, value.shape[0])


def join(parts):
    arrays, spans, rows = split(parts)
    return call(
        functools.partial(join_kernel, spans=spans),
        "join",
        array((rows, arrays[0].shape[1])),
        arrays,
        4,
        0,
    )


def pages_out_kernel(owner_ref, *refs, count):
    *blocks, rows, pages = refs
    blocks, outs = blocks[: -(count // 4)], blocks[-(count // 4) :]
    size = blocks[0].shape[0]
    page_len = outs[0].shape[0]
    seq_me, blk_me = lax.axis_index("seq"), lax.axis_index("blk")
    for k, block in enumerate(blocks):
        rows[pl.ds(pl.multiple_of((seq_me ^ k) * size, size), size)] = block[...]
    for j in range(count):
        step = owner_ref[0, j] ^ blk_me

        @pl.when(step % 4 == seq_me)
        def _(j=j, step=step):
            pages[count // 4 - 1 - step // 4] = rows[j * page_len : (j + 1) * page_len]

    for k, out in enumerate(outs):
        out[...] = pages[k]


def pages_out(owners, blocks):
    count = owners.shape[1]
    size, width = blocks[0].shape
    group_len = len(blocks) * size
    page_len = group_len // count
    return call(
        functools.partial(pages_out_kernel, count=count),
        "pages_out",
        (array((page_len, width)),) * (count // 4),
        (owners, *blocks),
        8,
        0,
        [pltpu.VMEM((group_len, width), BF16), pltpu.VMEM((count // 4, page_len, width), BF16)],
        scalars=1,
    )


def to_owner(page, number):
    seq_count, blk_count = lax.axis_size("seq"), lax.axis_size("blk")
    k = blk_count // 4 - 1 - number
    pairs = [
        (i * blk_count + b, i * blk_count + (b ^ (4 * k + i)))
        for i in range(seq_count)
        for b in range(blk_count)
    ]
    return lax.ppermute(page, ("seq", "blk"), pairs)


def cache_kernel(mine_ref, theirs_ref, gain_ref, w_ref, out_ref, rows, *, head_dim):
    count, page_len = out_ref.shape[1:3]
    seq_me, blk_me = lax.axis_index("seq"), lax.axis_index("blk")
    half = count // 4 * page_len
    for core, ref in enumerate((mine_ref, theirs_ref)):
        for chip in range(2):
            for k in range(count // 4):
                step = 4 * (count // 4 - 1 - k) + (seq_me ^ (2 * chip + core))
                start = (blk_me ^ step) * page_len
                page = ref[chip * half + k * page_len : chip * half + (k + 1) * page_len]
                rows[pl.ds(pl.multiple_of(start, page_len), page_len)] = page
    rows[...] = rms_norm(rows[...], gain_ref[0:1])
    for h in range(out_ref.shape[3] // (2 * head_dim)):
        columns = slice((3 * h + 1) * head_dim, 3 * (h + 1) * head_dim)
        out = jnp.dot(rows[...], w_ref[:, columns], preferred_element_type=F32).astype(BF16)
        out = out.reshape(count, page_len, 2 * head_dim)
        out_ref[0, :, :, 2 * h * head_dim : 2 * (h + 1) * head_dim] = out


def cache(mine, theirs, gains, w_flat, count, heads, head_dim):
    rows, width = mine.shape
    return call(
        functools.partial(cache_kernel, head_dim=head_dim),
        "cache",
        array((1, count, 2 * rows // count, heads * 2 * head_dim)),
        (mine, theirs, gains, w_flat),
        16,
        0,
        [pltpu.VMEM((2 * rows, width), BF16)],
    )


def pick_rows(pick, ffn_in, outs):
    picked = jnp.dot(pick, ffn_in, preferred_element_type=F32).astype(BF16)
    at = 0
    for out in outs:
        out[...] = picked[at : at + out.shape[0]]
        at += out.shape[0]


def dispatch_kernel(own_ref, mixed_ref, far_ref, gain_ref, pick_ref, resid_ref, ffn_ref, *outs):
    resid = own_ref[...].astype(F32) + mixed_ref[...] + far_ref[...].astype(F32)
    resid = resid.astype(BF16)
    resid_ref[...] = resid
    ffn_in = rms_norm(resid, gain_ref[1:2])
    ffn_ref[...] = ffn_in
    pick_rows(pick_ref[...], ffn_in, outs)


def dispatch(own, mixed, far, gains, pick, count):
    rows, width = own.shape
    capacity = pick.shape[0] // count
    return call(
        dispatch_kernel,
        "dispatch",
        (array((rows, width)),) * 2 + (array((capacity, width)),) * count,
        (own, mixed, far, gains, pick),
        max(10, pick.shape[0] * width * 12 >> 20),
        0,
    )


def dispatch_more_kernel(ffn_ref, pick_ref, *outs):
    pick_rows(pick_ref[...], ffn_ref[...], outs)


def dispatch_more(ffn_in, pick, sizes):
    width = ffn_in.shape[1]
    return call(
        dispatch_more_kernel,
        "dispatch_more",
        tuple(array((size, width)) for size in sizes),
        (ffn_in, pick),
        max(10, pick.shape[0] * width * 12 >> 20),
        1 << 34,
    )


def weigh_kernel(ffn_ref, router_ref, *refs, groups, sums):
    logits = lax.dot_general(
        router_ref[...], ffn_ref[...], (((1,), (1,)), ((), ())), preferred_element_type=F32
    )
    gates = jax.nn.sigmoid(logits).astype(BF16)
    experts = gates.shape[0]
    step = lax.broadcasted_iota(jnp.int32, (experts, experts), 0)
    expert = lax.broadcasted_iota(jnp.int32, (experts, experts), 1)
    order = jnp.where(lax.axis_index("blk") ^ step == expert, F32(1), F32(0)).astype(BF16)
    gates = jnp.dot(order, gates, preferred_element_type=F32)
    picks, outs = refs[: len(groups)], refs[len(groups) :]
    capacity = picks[0].shape[0] // len(groups[0])
    pick_of = {
        step: pick[i * capacity : (i + 1) * capacity]
        for group, pick in zip(groups, picks)
        for i, step in enumerate(group)
    }
    for steps, out in zip(sums, outs):
        parts = [pick_of[s].astype(F32) * gates[s : s + 1] for s in steps]
        out[...] = jnp.concatenate(parts, axis=0).T.astype(BF16)


def weigh(ffn_in, router, picks, groups, sums):
    capacity, rows = picks[0].shape[0] // len(groups[0]), ffn_in.shape[0]
    return call(
        functools.partial(weigh_kernel, groups=groups, sums=sums),
        "weigh",
        tuple(array((rows, len(steps) * capacity)) for steps in sums),
        (ffn_in, router, *picks),
        8,
        0,
    )


def expert_kernel(*refs, spans):
    count = len(spans)
    in_ref, down_ref = refs[count : count + 2]
    *outs, rows, hidden = refs[count + 2 :]
    ff, width = down_ref.shape
    join_rows(refs[:count], spans, rows)
    tile = min(ff, 512)
    for start in range(0, ff, tile):
        gate = jnp.dot(rows[...], in_ref[:, start : start + tile], preferred_element_type=F32)
        up = jnp.dot(
            rows[...], in_ref[:, ff + start : ff + start + tile], preferred_element_type=F32
        )
        hidden[:, start : start + tile] = (jax.nn.silu(gate) * up).astype(BF16)
    for start in range(0, width, tile):
        part = jnp.dot(hidden[...], down_ref[:, start : start + tile], preferred_element_type=F32)
        at = 0
        for out in outs:
            out[:, start : start + tile] = part[at : at + out.shape[0]].astype(BF16)
            at += out.shape[0]


def expert(parts, gate_up, down):
    arrays, spans, rows = split(parts)
    ff, width = down.shape
    return call(
        functools.partial(expert_kernel, spans=spans),
        "expert",
        tuple(array((high - low, width)) for low, high in spans),
        (*arrays, gate_up, down),
        max(8, rows * 20480 >> 20),
        1 << 35,
        [pltpu.VMEM((rows, width), BF16), pltpu.VMEM((rows, ff), BF16)],
    )


def combine_kernel(base_ref, weigh_ref, *refs, spans):
    *ins, out_ref, rows = refs
    join_rows(ins, spans, rows)
    total = jnp.dot(weigh_ref[...], rows[...], preferred_element_type=F32)
    out_ref[...] = (base_ref[...].astype(F32) + total).astype(out_ref.dtype)


def combine(base, weights, parts, dtype):
    arrays, spans, rows = split(parts)
    return call(
        functools.partial(combine_kernel, spans=spans),
        "combine",
        array(base.shape, dtype),
        (base, weights, *arrays),
        max(8, rows * 16384 >> 20),
        0,
        [pltpu.VMEM((rows, base.shape[1]), BF16)],
    )


def combine_last_kernel(base_ref, weigh_ref, *refs, spans):
    *ins, out_ref, rows, result, sems = refs
    join_rows(ins, spans, rows)
    tile = result.shape[1] // sems.shape[0]
    copies = []
    for n in range(sems.shape[0]):
        columns = slice(n * tile, (n + 1) * tile)
        total = jnp.dot(weigh_ref[...], rows[:, columns], preferred_element_type=F32)
        result[:, columns] = (base_ref[:, columns].astype(F32) + total).astype(BF16)
        window = pl.ds(n * tile, tile)
        copies.append(
            pltpu.make_async_copy(result.at[:, window], out_ref.at[0, :, window], sems.at[n])
        )
        copies[-1].start()
    for copy in copies:
        copy.wait()


def combine_last(base, weights, parts):
    arrays, spans, rows = split(parts)
    return pl.pallas_call(
        functools.partial(combine_last_kernel, spans=spans),
        out_shape=array((1,) + base.shape),
        in_specs=[VMEM_SPEC] * (2 + len(arrays)),
        out_specs=pl.BlockSpec(memory_space=pl.ANY),
        scratch_shapes=[
            pltpu.VMEM((rows, base.shape[1]), BF16),
            pltpu.VMEM(base.shape, BF16),
            pltpu.SemaphoreType.DMA((4,)),
        ],
        compiler_params=pltpu.CompilerParams(vmem_limit_bytes=max(8, rows * 16384 >> 20) << 20),
        cost_estimate=pl.CostEstimate(flops=0, bytes_accessed=0, transcendentals=0),
        name="combine_last",
    )(base, weights, *arrays)


def on_device(
    residual_in,
    segment_ids,
    attn_gain,
    w_qkv,
    w_out,
    ffn_gain,
    w_router,
    routes,
    w_gate_up,
    w_down,
    page_owner,
):
    own = residual_in[0]
    width = own.shape[1]
    heads_here = w_qkv.shape[1]
    head_dim = w_out.shape[1]
    blk_count = lax.axis_size("blk")

    slots = own.shape[0] * 3 // 8
    half = (4 + blk_count) // 2
    near, first, last = tuple(range(4)), tuple(range(4, half)), tuple(range(half, blk_count))
    groups = (first, (*near, *last))
    picks = plan(routes[0].T, groups)

    far = swap(own, "seq", 2)
    w_mine = w_out.reshape(heads_here * head_dim, width)
    core = swap(own, "seq", 1)
    w_theirs = swap(w_mine, "seq", 1)
    gains = jnp.stack([attn_gain, ffn_gain])

    w_flat = held(w_qkv.reshape(width, heads_here * 3 * head_dim))
    q_near, kv_near = project((own, core), gains, w_flat, heads_here, head_dim)
    far, q_near, kv_near = lax.optimization_barrier((far, q_near, kv_near))
    far_core = swap(far, "seq", 1)
    q_far, kv_far = project((far,), gains, w_flat, heads_here, head_dim)
    keep_far, send_far, kv_last = attend_far(
        segment_ids, q_far, kv_near, kv_far, far_core, gains, w_flat, head_dim
    )
    w_mine, w_theirs = held(w_mine), held(w_theirs)
    theirs_far = swap(send_far, "seq", 1)
    outgoing = pages_out(page_owner, (own, core, far, far_core))
    theirs_far, outgoing = lax.optimization_barrier((theirs_far, outgoing))
    far_sum = out_project(keep_far, theirs_far, w_mine, w_theirs, BF16)
    from_far = swap(far_sum, "seq", 2)
    keep, send = attend_near(segment_ids, q_near, (kv_near, kv_far, kv_last), head_dim)
    send, outgoing = lax.optimization_barrier((send, outgoing))
    arrived = [to_owner(page, k) for k, page in enumerate(outgoing)]
    mixed = out_project(keep, swap(send, "seq", 1), w_mine, w_theirs, F32)

    gate_up, down = held(w_gate_up[0]), held(w_down[0])

    def there(group, blocks):
        pairs = zip(group, blocks)
        return tuple(swap(block, "blk", step) if step else block for step, block in pairs)

    def work(blocks):
        return expert([full(block) for block in blocks], gate_up, down)

    resid, ffn_in, *sent_first = dispatch(own, mixed, from_far, gains, picks[0], len(first))
    rows_first = there(first, sent_first)
    sent = dispatch_more(ffn_in, picks[1], (slots,) * len(groups[1]))
    sent_near, sent_last = sent[: len(near)], sent[len(near) :]
    sent_near, arrived = lax.optimization_barrier((sent_near, arrived))
    rows_near = there(near, sent_near)
    share = join([full(page) for page in arrived])
    share_far = swap(share, "seq", 2)
    rows_last = there(last, sent_last)
    first_out = work(rows_first)
    back_first = there(first, first_out)
    rows_near, first_out, share_far = lax.optimization_barrier((rows_near, first_out, share_far))
    both = join([full(share), full(share_far)])
    both_core = swap(both, "seq", 1)
    near_out = work(rows_near)
    rows_last, both_core = lax.optimization_barrier((rows_last, both_core))
    last_out = work(rows_last)
    back_last = there(last, last_out)
    near_out, last_out, both_core = lax.optimization_barrier((near_out, last_out, both_core))
    back_near = there(near, near_out)
    kv_cache = cache(both, both_core, gains, w_flat, blk_count, heads_here, head_dim)

    weights = weigh(ffn_in, w_router.T, picks, groups, (first, (*last, *near)))
    total = combine(resid, weights[0], [full(block) for block in back_first], F32)
    kv_cache, total = lax.optimization_barrier((kv_cache, total))
    parts = [full(block) for block in (*back_last, *back_near)]
    residual_out = combine_last(total, weights[1], parts)
    return (residual_out, kv_cache)


def solution(mesh):
    in_specs = (
        P("blk", "seq", None),
        P("blk", None),
        P(),
        P(None, "seq", None),
        P("seq", None, None),
        P(),
        P(),
        P("blk", "seq", None),
        P("blk", None, None),
        P("blk", None, None),
        P("blk", None),
    )
    out_specs = (P("blk", "seq", None), P("blk", None, None, "seq"))
    return jax.shard_map(
        on_device, mesh=mesh, in_specs=in_specs, out_specs=out_specs, check_vma=False
    )
```

```python
import functools
import math

import jax
import jax.numpy as jnp
from jax import lax
from jax.experimental import pallas as pl
from jax.experimental.pallas import tpu as pltpu
from jax.sharding import PartitionSpec as P

EPS = 1e-06
F32 = jnp.float32
BF16 = jnp.bfloat16
VMEM_SPEC = pl.BlockSpec(memory_space=pltpu.VMEM)
SMEM_SPEC = pl.BlockSpec(memory_space=pltpu.SMEM)


def rms_norm(value, gain):
    wide = value.astype(F32)
    scale = lax.rsqrt(jnp.mean(wide * wide, axis=-1, keepdims=True) + EPS)
    return (wide * scale * gain.astype(F32)).astype(BF16)


def swap(value, axis, step):
    size = lax.axis_size(axis)
    return lax.ppermute(value, axis, [(i, i ^ step) for i in range(size)])


def held(value):
    return pltpu.with_memory_space_constraint(value, pltpu.VMEM)


def array(shape, dtype=BF16):
    return jax.ShapeDtypeStruct(shape, dtype)


def call(kernel, name, out_shape, args, mib, flops, scratch=(), scalars=0):
    return pl.pallas_call(
        kernel,
        out_shape=out_shape,
        in_specs=[SMEM_SPEC] * scalars + [VMEM_SPEC] * (len(args) - scalars),
        scratch_shapes=scratch,
        compiler_params=pltpu.CompilerParams(vmem_limit_bytes=mib << 20),
        cost_estimate=pl.CostEstimate(flops=flops, bytes_accessed=0, transcendentals=0),
        name=name,
    )(*args)


def plan_kernel(routes_ref, *outs, groups):
    top, rows = routes_ref.shape
    count = sum(map(len, groups))
    capacity = outs[0].shape[0] // len(groups[0])
    expert = lax.axis_index("blk") ^ lax.broadcasted_iota(jnp.int32, (count, rows), 0)
    chosen = jnp.zeros((count, rows), F32)
    for t in range(top):
        chosen = jnp.maximum(chosen, jnp.where(routes_ref[t : t + 1] == expert, F32(1), F32(0)))
    before = lax.broadcasted_iota(jnp.int32, (rows, rows), 0)
    after = lax.broadcasted_iota(jnp.int32, (rows, rows), 1)
    upto = jnp.where(before <= after, F32(1), F32(0)).astype(BF16)
    rank = jnp.dot(chosen.astype(BF16), upto, preferred_element_type=F32) - 1
    slot = jnp.where(chosen > 0, rank, F32(-1))
    place = lax.broadcasted_iota(jnp.int32, (capacity, rows), 0).astype(F32)
    for group, out in zip(groups, outs):
        for i, s in enumerate(group):
            hit = jnp.where(slot[s : s + 1] == place, F32(1), F32(0))
            out[i * capacity : (i + 1) * capacity] = hit.astype(BF16)


def plan(routes, groups):
    top, rows = routes.shape
    capacity = rows * 3 // 8
    return call(
        functools.partial(plan_kernel, groups=groups),
        "plan",
        tuple(array((len(group) * capacity, rows)) for group in groups),
        (routes,),
        4,
        0,
    )


def project_rows(blocks, gain_ref, w_ref, q_ref, kv_ref, normed, head_dim):
    rows = blocks[0].shape[0]
    for i, block in enumerate(blocks):
        normed[i * rows : (i + 1) * rows] = rms_norm(block[...], gain_ref[0:1])
    out = jnp.dot(normed[...], w_ref[...], preferred_element_type=F32).astype(BF16)
    for h in range(q_ref.shape[1] // head_dim):
        at = 3 * h * head_dim
        q_ref[:, h * head_dim : (h + 1) * head_dim] = out[:, at : at + head_dim]
        kv_ref[:, 2 * h * head_dim : 2 * (h + 1) * head_dim] = out[
            :, at + head_dim : at + 3 * head_dim
        ]


def project_kernel(*refs, head_dim):
    *blocks, gain_ref, w_ref, q_ref, kv_ref, normed = refs
    project_rows(blocks, gain_ref, w_ref, q_ref, kv_ref, normed, head_dim)


def project(blocks, gains, w_flat, heads, head_dim):
    rows, width = len(blocks) * blocks[0].shape[0], blocks[0].shape[1]
    return call(
        functools.partial(project_kernel, head_dim=head_dim),
        "project",
        (array((rows, heads * head_dim)), array((rows, heads * 2 * head_dim))),
        (*blocks, gains, w_flat),
        12,
        0,
        [pltpu.VMEM((rows, width), BF16)],
    )


def attend_rows(first, seg_ref, queries, kvs, keep_ref, send_ref, bias, head_dim):
    block = keep_ref.shape[0]
    me = lax.axis_index("seq")
    row = jnp.concatenate(
        [
            seg_ref[:, pl.ds(pl.multiple_of((me ^ k) * block, block), block)]
            for k in range(seg_ref.shape[1] // block)
        ],
        axis=1,
    ).astype(F32)
    column = jnp.broadcast_to(row, (8, row.shape[1])).T[first : first + 2 * block, 0:1]
    bias[...] = jnp.where(column == row, F32(0), F32(-1e30))
    factor = math.log2(math.e) / math.sqrt(head_dim)
    heads = range(queries[0].shape[1] // head_dim)
    columns = [slice(h * head_dim, (h + 1) * head_dim) for h in range(2 * len(heads))]

    def rows_of(refs, cols):
        return jnp.concatenate([ref[:, cols] for ref in refs], axis=0)

    scores = [
        lax.dot_general(
            rows_of(queries, columns[h]),
            rows_of(kvs, columns[2 * h]),
            (((1,), (1,)), ((), ())),
            preferred_element_type=F32,
        )
        for h in heads
    ]
    scores = [score + bias[...] for score in scores]
    tops = [jnp.max(score, axis=-1, keepdims=True) for score in scores]
    weights = [jnp.exp2((score - top) * factor) for score, top in zip(scores, tops)]
    totals = [jnp.sum(weight, axis=-1, keepdims=True) for weight in weights]
    for h in heads:
        value = rows_of(kvs, columns[2 * h + 1])
        context = jnp.dot(weights[h].astype(BF16), value, preferred_element_type=F32)
        context = (context / totals[h]).astype(BF16)
        keep_ref[:, columns[h]] = context[:block]
        send_ref[:, columns[h]] = context[block:]


def attend_near_kernel(seg, q, kv_near, kv_far, kv_last, keep, send, bias, *, head_dim):
    attend_rows(0, seg, [q], [kv_near, kv_far, kv_last], keep, send, bias, head_dim)


def attend_near(segments, q, kvs, head_dim):
    rows, cols = q.shape
    group_len = segments.shape[1]
    return call(
        functools.partial(attend_near_kernel, head_dim=head_dim),
        "attend_near",
        (array((rows // 2, cols)),) * 2,
        (segments, q, *kvs),
        12,
        1 << 34,
        [pltpu.VMEM((rows, group_len), F32)],
    )


def attend_far_kernel(
    seg, q_far, kv_near, kv_far, block, gain, w_ref, keep, send, kv, q, normed, bias, *, head_dim
):
    project_rows([block], gain, w_ref, q, kv, normed, head_dim)
    first = kv_near.shape[0]
    attend_rows(first, seg, [q_far, q], [kv_near, kv_far, kv], keep, send, bias, head_dim)


def attend_far(segments, q_far, kv_near, kv_far, block, gains, w_flat, head_dim):
    rows, cols = q_far.shape
    group_len = segments.shape[1]
    return call(
        functools.partial(attend_far_kernel, head_dim=head_dim),
        "attend_far",
        (array((rows, cols)),) * 2 + (array((rows, 2 * cols)),),
        (segments, q_far, kv_near, kv_far, block, gains, w_flat),
        12,
        0,
        [
            pltpu.VMEM((rows, cols), BF16),
            pltpu.VMEM(block.shape, BF16),
            pltpu.VMEM((2 * rows, group_len), F32),
        ],
    )


def out_project_kernel(mine_ref, theirs_ref, w_mine, w_theirs, out_ref):
    out = jnp.dot(mine_ref[...], w_mine[...], preferred_element_type=F32)
    out = out + jnp.dot(theirs_ref[...], w_theirs[...], preferred_element_type=F32)
    out_ref[...] = out.astype(out_ref.dtype)


def out_project(mine, theirs, w_mine, w_theirs, dtype):
    rows, depth = mine.shape
    width = w_mine.shape[1]
    return call(
        out_project_kernel,
        "out_project",
        array((rows, width), dtype),
        (mine, theirs, w_mine, w_theirs),
        8,
        0,
    )


def join_rows(refs, spans, out):
    at = 0
    for ref, (low, high) in zip(refs, spans):
        out[at : at + high - low] = ref[low:high]
        at += high - low


def join_kernel(*refs, spans):
    join_rows(refs[:-1], spans, refs[-1])


def split(parts):
    arrays = tuple(part[0] for part in parts)
    spans = tuple((low, high) for _, low, high in parts)
    return arrays, spans, sum(high - low for low, high in spans)


def full(value):
    return (value, 0, value.shape[0])


def join(parts):
    arrays, spans, rows = split(parts)
    return call(
        functools.partial(join_kernel, spans=spans),
        "join",
        array((rows, arrays[0].shape[1])),
        arrays,
        4,
        0,
    )


def pages_out_kernel(owner_ref, *refs, count):
    *blocks, rows, pages = refs
    blocks, outs = blocks[: -(count // 4)], blocks[-(count // 4) :]
    size = blocks[0].shape[0]
    page_len = outs[0].shape[0]
    seq_me, blk_me = lax.axis_index("seq"), lax.axis_index("blk")
    for k, block in enumerate(blocks):
        rows[pl.ds(pl.multiple_of((seq_me ^ k) * size, size), size)] = block[...]
    for j in range(count):
        step = owner_ref[0, j] ^ blk_me

        @pl.when(step % 4 == seq_me)
        def _(j=j, step=step):
            pages[count // 4 - 1 - step // 4] = rows[j * page_len : (j + 1) * page_len]

    for k, out in enumerate(outs):
        out[...] = pages[k]


def pages_out(owners, blocks):
    count = owners.shape[1]
    size, width = blocks[0].shape
    group_len = len(blocks) * size
    page_len = group_len // count
    return call(
        functools.partial(pages_out_kernel, count=count),
        "pages_out",
        (array((page_len, width)),) * (count // 4),
        (owners, *blocks),
        8,
        0,
        [pltpu.VMEM((group_len, width), BF16), pltpu.VMEM((count // 4, page_len, width), BF16)],
        scalars=1,
    )


def to_owner(page, number):
    seq_count, blk_count = lax.axis_size("seq"), lax.axis_size("blk")
    k = blk_count // 4 - 1 - number
    pairs = [
        (i * blk_count + b, i * blk_count + (b ^ (4 * k + i)))
        for i in range(seq_count)
        for b in range(blk_count)
    ]
    return lax.ppermute(page, ("seq", "blk"), pairs)


def cache_kernel(mine_ref, theirs_ref, gain_ref, w_ref, out_ref, rows, *, head_dim):
    count, page_len = out_ref.shape[1:3]
    seq_me, blk_me = lax.axis_index("seq"), lax.axis_index("blk")
    half = count // 4 * page_len
    for core, ref in enumerate((mine_ref, theirs_ref)):
        for chip in range(2):
            for k in range(count // 4):
                step = 4 * (count // 4 - 1 - k) + (seq_me ^ (2 * chip + core))
                start = (blk_me ^ step) * page_len
                page = ref[chip * half + k * page_len : chip * half + (k + 1) * page_len]
                rows[pl.ds(pl.multiple_of(start, page_len), page_len)] = page
    rows[...] = rms_norm(rows[...], gain_ref[0:1])
    for h in range(out_ref.shape[3] // (2 * head_dim)):
        columns = slice((3 * h + 1) * head_dim, 3 * (h + 1) * head_dim)
        out = jnp.dot(rows[...], w_ref[:, columns], preferred_element_type=F32).astype(BF16)
        out = out.reshape(count, page_len, 2 * head_dim)
        out_ref[0, :, :, 2 * h * head_dim : 2 * (h + 1) * head_dim] = out


def cache(mine, theirs, gains, w_flat, count, heads, head_dim):
    rows, width = mine.shape
    return call(
        functools.partial(cache_kernel, head_dim=head_dim),
        "cache",
        array((1, count, 2 * rows // count, heads * 2 * head_dim)),
        (mine, theirs, gains, w_flat),
        16,
        0,
        [pltpu.VMEM((2 * rows, width), BF16)],
    )


def pick_rows(pick, ffn_in, outs):
    picked = jnp.dot(pick, ffn_in, preferred_element_type=F32).astype(BF16)
    at = 0
    for out in outs:
        out[...] = picked[at : at + out.shape[0]]
        at += out.shape[0]


def dispatch_kernel(own_ref, mixed_ref, far_ref, gain_ref, pick_ref, resid_ref, ffn_ref, *outs):
    resid = own_ref[...].astype(F32) + mixed_ref[...] + far_ref[...].astype(F32)
    resid = resid.astype(BF16)
    resid_ref[...] = resid
    ffn_in = rms_norm(resid, gain_ref[1:2])
    ffn_ref[...] = ffn_in
    pick_rows(pick_ref[...], ffn_in, outs)


def dispatch(own, mixed, far, gains, pick, count):
    rows, width = own.shape
    capacity = pick.shape[0] // count
    return call(
        dispatch_kernel,
        "dispatch",
        (array((rows, width)),) * 2 + (array((capacity, width)),) * count,
        (own, mixed, far, gains, pick),
        max(10, pick.shape[0] * width * 12 >> 20),
        0,
    )


def dispatch_more_kernel(ffn_ref, pick_ref, *outs):
    pick_rows(pick_ref[...], ffn_ref[...], outs)


def dispatch_more(ffn_in, pick, sizes):
    width = ffn_in.shape[1]
    return call(
        dispatch_more_kernel,
        "dispatch_more",
        tuple(array((size, width)) for size in sizes),
        (ffn_in, pick),
        max(10, pick.shape[0] * width * 12 >> 20),
        1 << 34,
    )


def weigh_kernel(ffn_ref, router_ref, *refs, groups, sums):
    logits = lax.dot_general(
        router_ref[...], ffn_ref[...], (((1,), (1,)), ((), ())), preferred_element_type=F32
    )
    gates = jax.nn.sigmoid(logits).astype(BF16)
    experts = gates.shape[0]
    step = lax.broadcasted_iota(jnp.int32, (experts, experts), 0)
    expert = lax.broadcasted_iota(jnp.int32, (experts, experts), 1)
    order = jnp.where(lax.axis_index("blk") ^ step == expert, F32(1), F32(0)).astype(BF16)
    gates = jnp.dot(order, gates, preferred_element_type=F32)
    picks, outs = refs[: len(groups)], refs[len(groups) :]
    capacity = picks[0].shape[0] // len(groups[0])
    pick_of = {
        step: pick[i * capacity : (i + 1) * capacity]
        for group, pick in zip(groups, picks)
        for i, step in enumerate(group)
    }
    for steps, out in zip(sums, outs):
        parts = [pick_of[s].astype(F32) * gates[s : s + 1] for s in steps]
        out[...] = jnp.concatenate(parts, axis=0).T.astype(BF16)


def weigh(ffn_in, router, picks, groups, sums):
    capacity, rows = picks[0].shape[0] // len(groups[0]), ffn_in.shape[0]
    return call(
        functools.partial(weigh_kernel, groups=groups, sums=sums),
        "weigh",
        tuple(array((rows, len(steps) * capacity)) for steps in sums),
        (ffn_in, router, *picks),
        8,
        0,
    )


def expert_kernel(*refs, spans):
    count = len(spans)
    in_ref, down_ref = refs[count : count + 2]
    *outs, rows, hidden = refs[count + 2 :]
    ff, width = down_ref.shape
    join_rows(refs[:count], spans, rows)
    tile = min(ff, 512)
    for start in range(0, ff, tile):
        gate = jnp.dot(rows[...], in_ref[:, start : start + tile], preferred_element_type=F32)
        up = jnp.dot(
            rows[...], in_ref[:, ff + start : ff + start + tile], preferred_element_type=F32
        )
        hidden[:, start : start + tile] = (jax.nn.silu(gate) * up).astype(BF16)
    for start in range(0, width, tile):
        part = jnp.dot(hidden[...], down_ref[:, start : start + tile], preferred_element_type=F32)
        at = 0
        for out in outs:
            out[:, start : start + tile] = part[at : at + out.shape[0]].astype(BF16)
            at += out.shape[0]


def expert(parts, gate_up, down):
    arrays, spans, rows = split(parts)
    ff, width = down.shape
    return call(
        functools.partial(expert_kernel, spans=spans),
        "expert",
        tuple(array((high - low, width)) for low, high in spans),
        (*arrays, gate_up, down),
        max(8, rows * 20480 >> 20),
        1 << 35,
        [pltpu.VMEM((rows, width), BF16), pltpu.VMEM((rows, ff), BF16)],
    )


def combine_kernel(base_ref, weigh_ref, *refs, spans):
    *ins, out_ref, rows = refs
    join_rows(ins, spans, rows)
    total = jnp.dot(weigh_ref[...], rows[...], preferred_element_type=F32)
    out_ref[...] = (base_ref[...].astype(F32) + total).astype(out_ref.dtype)


def combine(base, weights, parts, dtype):
    arrays, spans, rows = split(parts)
    return call(
        functools.partial(combine_kernel, spans=spans),
        "combine",
        array(base.shape, dtype),
        (base, weights, *arrays),
        max(8, rows * 16384 >> 20),
        0,
        [pltpu.VMEM((rows, base.shape[1]), BF16)],
    )


def combine_last_kernel(base_ref, weigh_ref, *refs, spans):
    *ins, out_ref, rows, result, sems = refs
    join_rows(ins, spans, rows)
    tile = result.shape[1] // sems.shape[0]
    copies = []
    for n in range(sems.shape[0]):
        columns = slice(n * tile, (n + 1) * tile)
        total = jnp.dot(weigh_ref[...], rows[:, columns], preferred_element_type=F32)
        result[:, columns] = (base_ref[:, columns].astype(F32) + total).astype(BF16)
        window = pl.ds(n * tile, tile)
        copies.append(
            pltpu.make_async_copy(result.at[:, window], out_ref.at[0, :, window], sems.at[n])
        )
        copies[-1].start()
    for copy in copies:
        copy.wait()


def combine_last(base, weights, parts):
    arrays, spans, rows = split(parts)
    return pl.pallas_call(
        functools.partial(combine_last_kernel, spans=spans),
        out_shape=array((1,) + base.shape),
        in_specs=[VMEM_SPEC] * (2 + len(arrays)),
        out_specs=pl.BlockSpec(memory_space=pl.ANY),
        scratch_shapes=[
            pltpu.VMEM((rows, base.shape[1]), BF16),
            pltpu.VMEM(base.shape, BF16),
            pltpu.SemaphoreType.DMA((4,)),
        ],
        compiler_params=pltpu.CompilerParams(vmem_limit_bytes=max(8, rows * 16384 >> 20) << 20),
        cost_estimate=pl.CostEstimate(flops=0, bytes_accessed=0, transcendentals=0),
        name="combine_last",
    )(base, weights, *arrays)


def on_device(
    residual_in,
    segment_ids,
    attn_gain,
    w_qkv,
    w_out,
    ffn_gain,
    w_router,
    routes,
    w_gate_up,
    w_down,
    page_owner,
):
    own = residual_in[0]
    width = own.shape[1]
    heads_here = w_qkv.shape[1]
    head_dim = w_out.shape[1]
    blk_count = lax.axis_size("blk")

    slots = own.shape[0] * 3 // 8
    near = tuple(range(4))
    first, last = tuple(range(4, blk_count, 2)), tuple(range(5, blk_count, 2))
    groups = (first, (*near, *last))
    picks = plan(routes[0].T, groups)

    far = swap(own, "seq", 2)
    w_mine = w_out.reshape(heads_here * head_dim, width)
    core = swap(own, "seq", 1)
    w_theirs = swap(w_mine, "seq", 1)
    gains = jnp.stack([attn_gain, ffn_gain]).astype(F32)

    w_flat = held(w_qkv.reshape(width, heads_here * 3 * head_dim))
    q_near, kv_near = project((own, core), gains, w_flat, heads_here, head_dim)
    far, q_near, kv_near = lax.optimization_barrier((far, q_near, kv_near))
    far_core = swap(far, "seq", 1)
    q_far, kv_far = project((far,), gains, w_flat, heads_here, head_dim)
    keep_far, send_far, kv_last = attend_far(
        segment_ids, q_far, kv_near, kv_far, far_core, gains, w_flat, head_dim
    )
    w_mine, w_theirs = held(w_mine), held(w_theirs)
    theirs_far = swap(send_far, "seq", 1)
    outgoing = pages_out(page_owner, (own, core, far, far_core))
    theirs_far, outgoing = lax.optimization_barrier((theirs_far, outgoing))
    far_sum = out_project(keep_far, theirs_far, w_mine, w_theirs, BF16)
    from_far = swap(far_sum, "seq", 2)
    keep, send = attend_near(segment_ids, q_near, (kv_near, kv_far, kv_last), head_dim)
    send, outgoing = lax.optimization_barrier((send, outgoing))
    arrived = [to_owner(page, k) for k, page in enumerate(outgoing)]
    mixed = out_project(keep, swap(send, "seq", 1), w_mine, w_theirs, F32)

    gate_up, down = held(w_gate_up[0]), held(w_down[0])

    def there(group, blocks):
        pairs = zip(group, blocks)
        return tuple(swap(block, "blk", step) if step else block for step, block in pairs)

    def work(blocks):
        return expert([full(block) for block in blocks], gate_up, down)

    resid, ffn_in, *sent_first = dispatch(own, mixed, from_far, gains, picks[0], len(first))
    rows_first = there(first, sent_first)
    sent = dispatch_more(ffn_in, picks[1], (slots,) * len(groups[1]))
    sent_near, sent_last = sent[: len(near)], sent[len(near) :]
    sent_near, arrived = lax.optimization_barrier((sent_near, arrived))
    rows_near = there(near, sent_near)
    share = join([full(page) for page in arrived])
    share_far = swap(share, "seq", 2)
    rows_last = there(last, sent_last)
    first_out = work(rows_first)
    back_first = there(first, first_out)
    rows_near, first_out, share_far = lax.optimization_barrier((rows_near, first_out, share_far))
    both = join([full(share), full(share_far)])
    both_core = swap(both, "seq", 1)
    near_out = work(rows_near)
    rows_last, both_core = lax.optimization_barrier((rows_last, both_core))
    last_out = work(rows_last)
    back_last = there(last, last_out)
    back_near = there(near, near_out)
    kv_cache = cache(both, both_core, gains, w_flat, blk_count, heads_here, head_dim)

    weights = weigh(ffn_in, w_router.T, picks, groups, (first, (*last, *near)))
    total = combine(resid, weights[0], [full(block) for block in back_first], F32)
    kv_cache, total = lax.optimization_barrier((kv_cache, total))
    parts = [full(block) for block in (*back_last, *back_near)]
    residual_out = combine_last(total, weights[1], parts)
    return (residual_out, kv_cache)


def solution(mesh):
    in_specs = (
        P("blk", "seq", None),
        P("blk", None),
        P(),
        P(None, "seq", None),
        P("seq", None, None),
        P(),
        P(),
        P("blk", "seq", None),
        P("blk", None, None),
        P("blk", None, None),
        P("blk", None),
    )
    out_specs = (P("blk", "seq", None), P("blk", None, None, "seq"))
    return jax.shard_map(
        on_device, mesh=mesh, in_specs=in_specs, out_specs=out_specs, check_vma=False
    )
```

```python
import functools
import math

import jax
import jax.numpy as jnp
from jax import lax
from jax.experimental import pallas as pl
from jax.experimental.pallas import tpu as pltpu
from jax.sharding import PartitionSpec as P

EPS = 1e-06
F32 = jnp.float32
BF16 = jnp.bfloat16
VMEM_SPEC = pl.BlockSpec(memory_space=pltpu.VMEM)
SMEM_SPEC = pl.BlockSpec(memory_space=pltpu.SMEM)


def rms_norm(value, gain):
    wide = value.astype(F32)
    scale = lax.rsqrt(jnp.mean(wide * wide, axis=-1, keepdims=True) + EPS)
    return (wide * scale * gain.astype(F32)).astype(BF16)


def swap(value, axis, step):
    size = lax.axis_size(axis)
    return lax.ppermute(value, axis, [(i, i ^ step) for i in range(size)])


def held(value):
    return pltpu.with_memory_space_constraint(value, pltpu.VMEM)


def array(shape, dtype=BF16):
    return jax.ShapeDtypeStruct(shape, dtype)


def call(kernel, name, out_shape, args, mib, flops, scratch=(), scalars=0):
    return pl.pallas_call(
        kernel,
        out_shape=out_shape,
        in_specs=[SMEM_SPEC] * scalars + [VMEM_SPEC] * (len(args) - scalars),
        scratch_shapes=scratch,
        compiler_params=pltpu.CompilerParams(vmem_limit_bytes=mib << 20),
        cost_estimate=pl.CostEstimate(flops=flops, bytes_accessed=0, transcendentals=0),
        name=name,
    )(*args)


def plan_kernel(routes_ref, *outs, groups):
    top, rows = routes_ref.shape
    count = sum(map(len, groups))
    capacity = outs[0].shape[0] // len(groups[0])
    expert = lax.axis_index("blk") ^ lax.broadcasted_iota(jnp.int32, (count, rows), 0)
    chosen = jnp.zeros((count, rows), F32)
    for t in range(top):
        chosen = jnp.maximum(chosen, jnp.where(routes_ref[t : t + 1] == expert, F32(1), F32(0)))
    before = lax.broadcasted_iota(jnp.int32, (rows, rows), 0)
    after = lax.broadcasted_iota(jnp.int32, (rows, rows), 1)
    upto = jnp.where(before <= after, F32(1), F32(0)).astype(BF16)
    rank = jnp.dot(chosen.astype(BF16), upto, preferred_element_type=F32) - 1
    slot = jnp.where(chosen > 0, rank, F32(-1))
    place = lax.broadcasted_iota(jnp.int32, (capacity, rows), 0).astype(F32)
    for group, out in zip(groups, outs):
        for i, s in enumerate(group):
            hit = jnp.where(slot[s : s + 1] == place, F32(1), F32(0))
            out[i * capacity : (i + 1) * capacity] = hit.astype(BF16)


def plan(routes, groups):
    top, rows = routes.shape
    capacity = rows * 3 // 8
    return call(
        functools.partial(plan_kernel, groups=groups),
        "plan",
        tuple(array((len(group) * capacity, rows)) for group in groups),
        (routes,),
        4,
        0,
    )


def project_rows(blocks, gain_ref, w_ref, q_ref, kv_ref, normed, head_dim):
    rows = blocks[0].shape[0]
    for i, block in enumerate(blocks):
        normed[i * rows : (i + 1) * rows] = rms_norm(block[...], gain_ref[0:1])
    out = jnp.dot(normed[...], w_ref[...], preferred_element_type=F32).astype(BF16)
    for h in range(q_ref.shape[1] // head_dim):
        at = 3 * h * head_dim
        q_ref[:, h * head_dim : (h + 1) * head_dim] = out[:, at : at + head_dim]
        kv_ref[:, 2 * h * head_dim : 2 * (h + 1) * head_dim] = out[
            :, at + head_dim : at + 3 * head_dim
        ]


def project_kernel(*refs, head_dim):
    *blocks, gain_ref, w_ref, q_ref, kv_ref, normed = refs
    project_rows(blocks, gain_ref, w_ref, q_ref, kv_ref, normed, head_dim)


def project(blocks, gains, w_flat, heads, head_dim):
    rows, width = len(blocks) * blocks[0].shape[0], blocks[0].shape[1]
    return call(
        functools.partial(project_kernel, head_dim=head_dim),
        "project",
        (array((rows, heads * head_dim)), array((rows, heads * 2 * head_dim))),
        (*blocks, gains, w_flat),
        12,
        0,
        [pltpu.VMEM((rows, width), BF16)],
    )


def attend_rows(first, seg_ref, queries, kvs, keep_ref, send_ref, bias, head_dim):
    block = keep_ref.shape[0]
    me = lax.axis_index("seq")
    row = jnp.concatenate(
        [
            seg_ref[:, pl.ds(pl.multiple_of((me ^ k) * block, block), block)]
            for k in range(seg_ref.shape[1] // block)
        ],
        axis=1,
    ).astype(F32)
    column = jnp.broadcast_to(row, (8, row.shape[1])).T[first : first + 2 * block, 0:1]
    bias[...] = jnp.where(column == row, F32(0), F32(-1e30))
    factor = math.log2(math.e) / math.sqrt(head_dim)
    heads = range(queries[0].shape[1] // head_dim)
    columns = [slice(h * head_dim, (h + 1) * head_dim) for h in range(2 * len(heads))]

    def rows_of(refs, cols):
        return jnp.concatenate([ref[:, cols] for ref in refs], axis=0)

    scores = [
        lax.dot_general(
            rows_of(queries, columns[h]),
            rows_of(kvs, columns[2 * h]),
            (((1,), (1,)), ((), ())),
            preferred_element_type=F32,
        )
        for h in heads
    ]
    scores = [score + bias[...] for score in scores]
    tops = [jnp.max(score, axis=-1, keepdims=True) for score in scores]
    weights = [jnp.exp2((score - top) * factor) for score, top in zip(scores, tops)]
    ones = jnp.ones((row.shape[1], head_dim), BF16)
    for h in heads:
        value = jnp.concatenate([rows_of(kvs, columns[2 * h + 1]), ones], axis=1)
        context = jnp.dot(weights[h].astype(BF16), value, preferred_element_type=F32)
        context = (context[:, :head_dim] / context[:, head_dim:]).astype(BF16)
        keep_ref[:, columns[h]] = context[:block]
        send_ref[:, columns[h]] = context[block:]


def attend_near_kernel(seg, q, kv_near, kv_far, kv_last, keep, send, bias, *, head_dim):
    attend_rows(0, seg, [q], [kv_near, kv_far, kv_last], keep, send, bias, head_dim)


def attend_near(segments, q, kvs, head_dim):
    rows, cols = q.shape
    group_len = segments.shape[1]
    return call(
        functools.partial(attend_near_kernel, head_dim=head_dim),
        "attend_near",
        (array((rows // 2, cols)),) * 2,
        (segments, q, *kvs),
        12,
        1 << 34,
        [pltpu.VMEM((rows, group_len), F32)],
    )


def attend_far_kernel(
    seg, q_far, kv_near, kv_far, block, gain, w_ref, keep, send, kv, q, normed, bias, *, head_dim
):
    project_rows([block], gain, w_ref, q, kv, normed, head_dim)
    first = kv_near.shape[0]
    attend_rows(first, seg, [q_far, q], [kv_near, kv_far, kv], keep, send, bias, head_dim)


def attend_far(segments, q_far, kv_near, kv_far, block, gains, w_flat, head_dim):
    rows, cols = q_far.shape
    group_len = segments.shape[1]
    return call(
        functools.partial(attend_far_kernel, head_dim=head_dim),
        "attend_far",
        (array((rows, cols)),) * 2 + (array((rows, 2 * cols)),),
        (segments, q_far, kv_near, kv_far, block, gains, w_flat),
        12,
        0,
        [
            pltpu.VMEM((rows, cols), BF16),
            pltpu.VMEM(block.shape, BF16),
            pltpu.VMEM((2 * rows, group_len), F32),
        ],
    )


def out_project_kernel(mine_ref, theirs_ref, w_mine, w_theirs, out_ref):
    out = jnp.dot(mine_ref[...], w_mine[...], preferred_element_type=F32)
    out = out + jnp.dot(theirs_ref[...], w_theirs[...], preferred_element_type=F32)
    out_ref[...] = out.astype(out_ref.dtype)


def out_project(mine, theirs, w_mine, w_theirs, dtype):
    rows, depth = mine.shape
    width = w_mine.shape[1]
    return call(
        out_project_kernel,
        "out_project",
        array((rows, width), dtype),
        (mine, theirs, w_mine, w_theirs),
        8,
        0,
    )


def join_rows(refs, spans, out):
    at = 0
    for ref, (low, high) in zip(refs, spans):
        out[at : at + high - low] = ref[low:high]
        at += high - low


def join_kernel(*refs, spans):
    join_rows(refs[:-1], spans, refs[-1])


def split(parts):
    arrays = tuple(part[0] for part in parts)
    spans = tuple((low, high) for _, low, high in parts)
    return arrays, spans, sum(high - low for low, high in spans)


def full(value):
    return (value, 0, value.shape[0])


def join(parts):
    arrays, spans, rows = split(parts)
    return call(
        functools.partial(join_kernel, spans=spans),
        "join",
        array((rows, arrays[0].shape[1])),
        arrays,
        4,
        0,
    )


def pages_out_kernel(owner_ref, *refs, count):
    *blocks, rows, pages = refs
    blocks, outs = blocks[: -(count // 4)], blocks[-(count // 4) :]
    size = blocks[0].shape[0]
    page_len = outs[0].shape[0]
    seq_me, blk_me = lax.axis_index("seq"), lax.axis_index("blk")
    for k, block in enumerate(blocks):
        rows[pl.ds(pl.multiple_of((seq_me ^ k) * size, size), size)] = block[...]
    for j in range(count):
        step = owner_ref[0, j] ^ blk_me

        @pl.when(step % 4 == seq_me)
        def _(j=j, step=step):
            pages[count // 4 - 1 - step // 4] = rows[j * page_len : (j + 1) * page_len]

    for k, out in enumerate(outs):
        out[...] = pages[k]


def pages_out(owners, blocks):
    count = owners.shape[1]
    size, width = blocks[0].shape
    group_len = len(blocks) * size
    page_len = group_len // count
    return call(
        functools.partial(pages_out_kernel, count=count),
        "pages_out",
        (array((page_len, width)),) * (count // 4),
        (owners, *blocks),
        8,
        0,
        [pltpu.VMEM((group_len, width), BF16), pltpu.VMEM((count // 4, page_len, width), BF16)],
        scalars=1,
    )


def to_owner(page, number):
    seq_count, blk_count = lax.axis_size("seq"), lax.axis_size("blk")
    k = blk_count // 4 - 1 - number
    pairs = [
        (i * blk_count + b, i * blk_count + (b ^ (4 * k + i)))
        for i in range(seq_count)
        for b in range(blk_count)
    ]
    return lax.ppermute(page, ("seq", "blk"), pairs)


def cache_kernel(mine_ref, theirs_ref, gain_ref, w_ref, out_ref, rows, *, head_dim):
    count, page_len = out_ref.shape[1:3]
    seq_me, blk_me = lax.axis_index("seq"), lax.axis_index("blk")
    half = count // 4 * page_len
    for core, ref in enumerate((mine_ref, theirs_ref)):
        for chip in range(2):
            for k in range(count // 4):
                step = 4 * (count // 4 - 1 - k) + (seq_me ^ (2 * chip + core))
                start = (blk_me ^ step) * page_len
                page = ref[chip * half + k * page_len : chip * half + (k + 1) * page_len]
                rows[pl.ds(pl.multiple_of(start, page_len), page_len)] = page
    rows[...] = rms_norm(rows[...], gain_ref[0:1])
    for h in range(out_ref.shape[3] // (2 * head_dim)):
        columns = slice((3 * h + 1) * head_dim, 3 * (h + 1) * head_dim)
        out = jnp.dot(rows[...], w_ref[:, columns], preferred_element_type=F32).astype(BF16)
        out = out.reshape(count, page_len, 2 * head_dim)
        out_ref[0, :, :, 2 * h * head_dim : 2 * (h + 1) * head_dim] = out


def cache(mine, theirs, gains, w_flat, count, heads, head_dim):
    rows, width = mine.shape
    return call(
        functools.partial(cache_kernel, head_dim=head_dim),
        "cache",
        array((1, count, 2 * rows // count, heads * 2 * head_dim)),
        (mine, theirs, gains, w_flat),
        16,
        0,
        [pltpu.VMEM((2 * rows, width), BF16)],
    )


def pick_rows(pick, ffn_in, outs):
    picked = jnp.dot(pick, ffn_in, preferred_element_type=F32).astype(BF16)
    at = 0
    for out in outs:
        out[...] = picked[at : at + out.shape[0]]
        at += out.shape[0]


def dispatch_kernel(own_ref, mixed_ref, far_ref, gain_ref, pick_ref, resid_ref, ffn_ref, *outs):
    resid = own_ref[...].astype(F32) + mixed_ref[...] + far_ref[...].astype(F32)
    resid = resid.astype(BF16)
    resid_ref[...] = resid
    ffn_in = rms_norm(resid, gain_ref[1:2])
    ffn_ref[...] = ffn_in
    pick_rows(pick_ref[...], ffn_in, outs)


def dispatch(own, mixed, far, gains, pick, count):
    rows, width = own.shape
    capacity = pick.shape[0] // count
    return call(
        dispatch_kernel,
        "dispatch",
        (array((rows, width)),) * 2 + (array((capacity, width)),) * count,
        (own, mixed, far, gains, pick),
        max(10, pick.shape[0] * width * 12 >> 20),
        0,
    )


def dispatch_more_kernel(ffn_ref, pick_ref, *outs):
    pick_rows(pick_ref[...], ffn_ref[...], outs)


def dispatch_more(ffn_in, pick, sizes):
    width = ffn_in.shape[1]
    return call(
        dispatch_more_kernel,
        "dispatch_more",
        tuple(array((size, width)) for size in sizes),
        (ffn_in, pick),
        max(10, pick.shape[0] * width * 12 >> 20),
        1 << 34,
    )


def weigh_kernel(ffn_ref, router_ref, *refs, groups, sums):
    logits = lax.dot_general(
        router_ref[...], ffn_ref[...], (((1,), (1,)), ((), ())), preferred_element_type=F32
    )
    gates = jax.nn.sigmoid(logits).astype(BF16)
    experts = gates.shape[0]
    step = lax.broadcasted_iota(jnp.int32, (experts, experts), 0)
    expert = lax.broadcasted_iota(jnp.int32, (experts, experts), 1)
    order = jnp.where(lax.axis_index("blk") ^ step == expert, F32(1), F32(0)).astype(BF16)
    gates = jnp.dot(order, gates, preferred_element_type=F32)
    picks, outs = refs[: len(groups)], refs[len(groups) :]
    capacity = picks[0].shape[0] // len(groups[0])
    pick_of = {
        step: pick[i * capacity : (i + 1) * capacity]
        for group, pick in zip(groups, picks)
        for i, step in enumerate(group)
    }
    for steps, out in zip(sums, outs):
        parts = [pick_of[s].astype(F32) * gates[s : s + 1] for s in steps]
        out[...] = jnp.concatenate(parts, axis=0).T.astype(BF16)


def weigh(ffn_in, router, picks, groups, sums):
    capacity, rows = picks[0].shape[0] // len(groups[0]), ffn_in.shape[0]
    return call(
        functools.partial(weigh_kernel, groups=groups, sums=sums),
        "weigh",
        tuple(array((rows, len(steps) * capacity)) for steps in sums),
        (ffn_in, router, *picks),
        8,
        0,
    )


def expert_kernel(*refs, spans):
    count = len(spans)
    in_ref, down_ref = refs[count : count + 2]
    *outs, rows, hidden = refs[count + 2 :]
    ff, width = down_ref.shape
    join_rows(refs[:count], spans, rows)
    tile = min(ff, 512)
    for start in range(0, ff, tile):
        gate = jnp.dot(rows[...], in_ref[:, start : start + tile], preferred_element_type=F32)
        up = jnp.dot(
            rows[...], in_ref[:, ff + start : ff + start + tile], preferred_element_type=F32
        )
        hidden[:, start : start + tile] = (jax.nn.silu(gate) * up).astype(BF16)
    for start in range(0, width, tile):
        part = jnp.dot(hidden[...], down_ref[:, start : start + tile], preferred_element_type=F32)
        at = 0
        for out in outs:
            out[:, start : start + tile] = part[at : at + out.shape[0]].astype(BF16)
            at += out.shape[0]


def expert(parts, gate_up, down):
    arrays, spans, rows = split(parts)
    ff, width = down.shape
    return call(
        functools.partial(expert_kernel, spans=spans),
        "expert",
        tuple(array((high - low, width)) for low, high in spans),
        (*arrays, gate_up, down),
        max(8, rows * 20480 >> 20),
        1 << 35,
        [pltpu.VMEM((rows, width), BF16), pltpu.VMEM((rows, ff), BF16)],
    )


def combine_kernel(base_ref, weigh_ref, *refs, spans):
    *ins, out_ref, rows = refs
    join_rows(ins, spans, rows)
    total = jnp.dot(weigh_ref[...], rows[...], preferred_element_type=F32)
    out_ref[...] = (base_ref[...].astype(F32) + total).astype(out_ref.dtype)


def combine(base, weights, parts, dtype):
    arrays, spans, rows = split(parts)
    return call(
        functools.partial(combine_kernel, spans=spans),
        "combine",
        array(base.shape, dtype),
        (base, weights, *arrays),
        max(8, rows * 16384 >> 20),
        0,
        [pltpu.VMEM((rows, base.shape[1]), BF16)],
    )


def combine_last_kernel(base_ref, weigh_ref, *refs, spans):
    *ins, out_ref, rows, result, sems = refs
    join_rows(ins, spans, rows)
    tile = result.shape[1] // sems.shape[0]
    copies = []
    for n in range(sems.shape[0]):
        columns = slice(n * tile, (n + 1) * tile)
        total = jnp.dot(weigh_ref[...], rows[:, columns], preferred_element_type=F32)
        result[:, columns] = (base_ref[:, columns].astype(F32) + total).astype(BF16)
        window = pl.ds(n * tile, tile)
        copies.append(
            pltpu.make_async_copy(result.at[:, window], out_ref.at[0, :, window], sems.at[n])
        )
        copies[-1].start()
    for copy in copies:
        copy.wait()


def combine_last(base, weights, parts):
    arrays, spans, rows = split(parts)
    return pl.pallas_call(
        functools.partial(combine_last_kernel, spans=spans),
        out_shape=array((1,) + base.shape),
        in_specs=[VMEM_SPEC] * (2 + len(arrays)),
        out_specs=pl.BlockSpec(memory_space=pl.ANY),
        scratch_shapes=[
            pltpu.VMEM((rows, base.shape[1]), BF16),
            pltpu.VMEM(base.shape, BF16),
            pltpu.SemaphoreType.DMA((4,)),
        ],
        compiler_params=pltpu.CompilerParams(vmem_limit_bytes=max(8, rows * 16384 >> 20) << 20),
        cost_estimate=pl.CostEstimate(flops=0, bytes_accessed=0, transcendentals=0),
        name="combine_last",
    )(base, weights, *arrays)


def on_device(
    residual_in,
    segment_ids,
    attn_gain,
    w_qkv,
    w_out,
    ffn_gain,
    w_router,
    routes,
    w_gate_up,
    w_down,
    page_owner,
):
    own = residual_in[0]
    width = own.shape[1]
    heads_here = w_qkv.shape[1]
    head_dim = w_out.shape[1]
    blk_count = lax.axis_size("blk")

    slots = own.shape[0] * 3 // 8
    near = tuple(range(4))
    first, last = tuple(range(4, blk_count, 2)), tuple(range(5, blk_count, 2))
    groups = (first, (*near, *last))
    picks = plan(routes[0].T, groups)

    far = swap(own, "seq", 2)
    w_mine = w_out.reshape(heads_here * head_dim, width)
    core = swap(own, "seq", 1)
    w_theirs = swap(w_mine, "seq", 1)
    gains = jnp.stack([attn_gain, ffn_gain]).astype(F32)

    w_flat = held(w_qkv.reshape(width, heads_here * 3 * head_dim))
    q_near, kv_near = project((own, core), gains, w_flat, heads_here, head_dim)
    far, q_near, kv_near = lax.optimization_barrier((far, q_near, kv_near))
    far_core = swap(far, "seq", 1)
    q_far, kv_far = project((far,), gains, w_flat, heads_here, head_dim)
    keep_far, send_far, kv_last = attend_far(
        segment_ids, q_far, kv_near, kv_far, far_core, gains, w_flat, head_dim
    )
    w_mine, w_theirs = held(w_mine), held(w_theirs)
    theirs_far = swap(send_far, "seq", 1)
    outgoing = pages_out(page_owner, (own, core, far, far_core))
    theirs_far, outgoing = lax.optimization_barrier((theirs_far, outgoing))
    far_sum = out_project(keep_far, theirs_far, w_mine, w_theirs, BF16)
    from_far = swap(far_sum, "seq", 2)
    keep, send = attend_near(segment_ids, q_near, (kv_near, kv_far, kv_last), head_dim)
    send, outgoing = lax.optimization_barrier((send, outgoing))
    arrived = [to_owner(page, k) for k, page in enumerate(outgoing)]
    mixed = out_project(keep, swap(send, "seq", 1), w_mine, w_theirs, F32)

    gate_up, down = held(w_gate_up[0]), held(w_down[0])

    def there(group, blocks):
        pairs = zip(group, blocks)
        return tuple(swap(block, "blk", step) if step else block for step, block in pairs)

    def work(blocks):
        return expert([full(block) for block in blocks], gate_up, down)

    resid, ffn_in, *sent_first = dispatch(own, mixed, from_far, gains, picks[0], len(first))
    rows_first = there(first, sent_first)
    sent = dispatch_more(ffn_in, picks[1], (slots,) * len(groups[1]))
    sent_near, sent_last = sent[: len(near)], sent[len(near) :]
    sent_near, arrived = lax.optimization_barrier((sent_near, arrived))
    rows_near = there(near, sent_near)
    share = join([full(page) for page in arrived])
    share_far = swap(share, "seq", 2)
    rows_last = there(last, sent_last)
    first_out = work(rows_first)
    back_first = there(first, first_out)
    rows_near, first_out, share_far = lax.optimization_barrier((rows_near, first_out, share_far))
    both = join([full(share), full(share_far)])
    both_core = swap(both, "seq", 1)
    near_out = work(rows_near)
    rows_last, both_core = lax.optimization_barrier((rows_last, both_core))
    last_out = work(rows_last)
    back_last = there(last, last_out)
    back_near = there(near, near_out)
    kv_cache = cache(both, both_core, gains, w_flat, blk_count, heads_here, head_dim)

    weights = weigh(ffn_in, w_router.T, picks, groups, (first, (*last, *near)))
    total = combine(resid, weights[0], [full(block) for block in back_first], F32)
    kv_cache, total = lax.optimization_barrier((kv_cache, total))
    parts = [full(block) for block in (*back_last, *back_near)]
    residual_out = combine_last(total, weights[1], parts)
    return (residual_out, kv_cache)


def solution(mesh):
    in_specs = (
        P("blk", "seq", None),
        P("blk", None),
        P(),
        P(None, "seq", None),
        P("seq", None, None),
        P(),
        P(),
        P("blk", "seq", None),
        P("blk", None, None),
        P("blk", None, None),
        P("blk", None),
    )
    out_specs = (P("blk", "seq", None), P("blk", None, None, "seq"))
    return jax.shard_map(
        on_device, mesh=mesh, in_specs=in_specs, out_specs=out_specs, check_vma=False
    )
```
